128 devices in a mesh: occ: 8 (over z_lo, y), vir: 16 (over x, z_hi, core).
Axes of the slice: x: 4, y: 4, z: 4 (z_hi: 2, z_lo: 2; z = z_hi * 2 + z_lo), core: 2. Of those that a mesh axis runs over, the one named last changes fastest.
Arguments:
- lam: bfloat16 [8192, 28672], P('occ', 'vir'), may hold values from -6 to 6
- ladder_int: bfloat16 [28672, 4096], P('vir'), may hold values from -0.046875 to 0.046875
- cycle_amp: bfloat16 [1024, 3200], P('occ'), may hold values from -6 to 6
- cycle_int: bfloat16 [3200, 32768], P('occ', 'vir'), may hold values from -0.3125 to 0.3125
- occ_irrep: int32 [200], replicated, may hold values from 0 to 7, as said below
- virt_irrep: int32 [256], replicated, may hold values from 0 to 7, as said below
Outputs:
- residual: float32 [1024, 32768], P('occ', 'vir')
The draws below stay inside these ranges and needn't reach their ends.
Inputs may be any that keep to these rules, and one draw needn't show every extreme that they name: `occ_irrep`: nondecreasing along the orbitals (contiguous symmetry blocks); every label 0 to 7 occurs. `virt_irrep`: nondecreasing along the orbitals (contiguous symmetry blocks); every label 0 to 7 occurs.
All inputs are finite; a program needn't handle non-finite values.
Results may differ from the reference program's by a relative error of at most 0.0003.
Values may be sent and summed in bfloat16 or wider, within the bound.
No kernel may reach another device: no remote copies, remote signals or barrier semaphores. Data moves between devices by JAX's collectives and lax.ppermute only.
A program may use at most 128 MiB of HBM per device.

```python
import jax
import jax.numpy as jnp

VIRT = 1792
KOCC = 200
PAN = 16
AW = 16
BW = 256
JW = 128
IW = 64


def sorted_labels(key, length):
    extra = jax.random.randint(key, (length - 8,), 0, 8, dtype=jnp.int32)
    return jnp.sort(jnp.concatenate([jnp.arange(8, dtype=jnp.int32), extra]))


def draw_occ_irrep(key, part):
    key = jax.random.fold_in(key, 11)
    return sorted_labels(key, KOCC)


def draw_virt_irrep(key, part):
    key = jax.random.fold_in(key, 23)
    return sorted_labels(key, BW)


def with_spikes(drawn, key, source, target, blocks, factor):
    def block_of(position):
        return (jnp.arange(drawn.shape[position]) // (drawn.shape[position] // blocks)).reshape((-1,) + (1,) * (drawn.ndim - 1 - position))

    near = jax.random.permutation(key, blocks)[block_of(target)]
    other_side = (block_of(target) + blocks // 2) % blocks
    return jnp.where((block_of(source) == near) | (block_of(source) == other_side), factor * drawn, drawn)


def shard_levels(key, shape, cuts, low, top_value):
    gain, own = 1.0, jax.random.fold_in(key, 6)
    for dim, blocks in cuts:
        draws = jnp.exp(jax.random.uniform(jax.random.fold_in(own, dim), (blocks,), jnp.float32, low / len(cuts), top_value / len(cuts)))
        gain = gain * jnp.repeat(draws, shape[dim] // blocks).reshape([-1 if axis == dim else 1 for axis in range(len(shape))])
    return gain


def centred(key, dims, deviation, limit, split=(), kind=jnp.bfloat16):
    result = deviation * jax.random.normal(key, dims, jnp.float32)
    if split:
        result = result * shard_levels(key, dims, split, -0.22, 0.18)
    return jnp.clip(result, -limit, limit).astype(kind)


def heavy_noise(key, dims, spread, most, shards, heavy, held_as=jnp.bfloat16):
    values = spread * jax.random.normal(key, dims, jnp.float32)
    if shards:
        values = values * shard_levels(key, dims, shards, -0.22, 0.18)
    return jnp.clip(with_spikes(values, jax.random.fold_in(key, 3), *heavy), -most, most).astype(held_as)


def setup_inputs(seed: int = 0) -> dict:
    streams_of = jax.random.split(jax.random.key(seed), 7)
    return {
        "lam": centred(streams_of[0], (IW * JW, PAN * VIRT), 1.0, 6.0, ((0, 8), (1, 16))),
        "ladder_int": heavy_noise(streams_of[1], (PAN * VIRT, AW * BW), (PAN * VIRT) ** -0.5, 0.046875, ((0, 16),), (0, 1, 16, 2.0)),
        "cycle_amp": centred(streams_of[2], (IW * AW, KOCC * PAN), 1.0, 6.0, ((0, 8),)),
        "cycle_int": centred(streams_of[3], (KOCC * PAN, JW * BW), (KOCC * PAN // 8) ** -0.5, 0.3125, ((0, 8), (1, 16))),
        "occ_irrep": draw_occ_irrep(jax.random.fold_in(streams_of[6], 71), 0),
        "virt_irrep": draw_virt_irrep(jax.random.fold_in(streams_of[6], 71), 0),
    }


def reference(lam, ladder_int, cycle_amp, cycle_int, occ_irrep, virt_irrep):
    ladder = jnp.dot(lam, ladder_int, preferred_element_type=jnp.float32)
    regrouped = ladder.reshape(IW, JW, AW, BW).transpose(0, 2, 1, 3).reshape(IW * AW, JW * BW)
    kc_irrep = (occ_irrep[:, None] ^ virt_irrep[None, :PAN]).reshape(-1)
    jb_irrep = (occ_irrep[:JW, None] ^ virt_irrep[None, :]).reshape(-1)
    masked = jnp.where(kc_irrep[:, None] == jb_irrep[None, :], cycle_int, jnp.zeros((), cycle_int.dtype))
    cycle = jnp.dot(cycle_amp, masked, preferred_element_type=jnp.float32)
    return regrouped + cycle
```

```python
import functools

import jax
import jax.numpy as jnp
from jax import lax
from jax.experimental import pallas as pl
from jax.experimental.pallas import tpu as pltpu
from jax.sharding import Mesh, PartitionSpec as P

PAN = 16
AW = 16
BW = 256
JW = 128
LANES = 128
SCALE_ROWS = 16
SEGMENT = 64
Z_COLUMNS = 2048
TILE = 512
VMEM_BYTES = 56 * 1024 * 1024

VIR = ("x", "z_hi", "core")
OCC = ("z_lo", "y")


def encode(block):
    top = jnp.maximum(jnp.max(jnp.abs(block), axis=0, keepdims=True), 1e-30)
    level = jnp.ceil(jnp.log2(top) * 256.0) + 1.0
    step = jnp.exp2(level * (-1.0 / 256.0)) * 32767.0
    return jnp.round(block * step).astype(jnp.int32).astype(jnp.int16), level


def decode(code, level):
    step = jnp.exp2(level * (1.0 / 256.0)) * (1.0 / 32767.0)
    return code.astype(jnp.int32).astype(jnp.float32) * step


def level_rows(levels):
    spare = jnp.zeros((1, LANES), jnp.float32)
    rows = jnp.concatenate(levels + [spare] * (SCALE_ROWS - len(levels)), axis=0)
    return rows.astype(jnp.int32).astype(jnp.int16)


def read_levels(block):
    return block.astype(jnp.int32).astype(jnp.float32)


def params(**more):
    return pltpu.CompilerParams(vmem_limit_bytes=VMEM_BYTES, **more)


def cost(rows, depth, columns, more=0):
    return pl.CostEstimate(
        flops=2 * rows * depth * columns,
        bytes_accessed=2 * (rows * depth + depth * columns) + more,
        transcendentals=0,
    )


def columns_of(block):
    return pl.ds(block * LANES, LANES)


def partner_kernel(lam_ref, panel_ref, out_ref):
    rows = lam_ref.shape[0]
    acc = jnp.dot(lam_ref[...], panel_ref[...], preferred_element_type=jnp.float32)
    blocks = acc.shape[1] // LANES
    levels = []
    for block in range(blocks):
        code, level = encode(acc[:, block * LANES : (block + 1) * LANES])
        out_ref[0, block * rows : (block + 1) * rows, :] = code
        levels.append(level)
    out_ref[0, blocks * rows :, :] = level_rows(levels)


def partner_part(lam_rows, panel, first, width):
    rows, depth = lam_rows.shape
    tiles, offset = width // TILE, first // TILE
    size = TILE // LANES * rows + SCALE_ROWS
    return pl.pallas_call(
        partner_kernel,
        grid=(tiles,),
        in_specs=[
            pl.BlockSpec((rows, depth), lambda t: (0, 0)),
            pl.BlockSpec((depth, TILE), lambda t: (0, t + offset)),
        ],
        out_specs=pl.BlockSpec((1, size, LANES), lambda t: (t, 0, 0)),
        out_shape=jax.ShapeDtypeStruct((tiles, size, LANES), jnp.int16),
        compiler_params=params(),
        cost_estimate=cost(rows, depth, width),
        name="partner_part",
    )(lam_rows, panel)


def own_sum(lam_ref, panel_ref, recv_ref):
    rows = lam_ref.shape[0]
    acc = jnp.dot(lam_ref[...], panel_ref[...], preferred_element_type=jnp.float32)
    blocks = acc.shape[1] // LANES
    levels = read_levels(recv_ref[0, blocks * rows :, :])
    sums = []
    for block in range(blocks):
        got = decode(recv_ref[0, block * rows : (block + 1) * rows, :], levels[block : block + 1, :])
        sums.append(acc[:, block * LANES : (block + 1) * LANES] + got)
    return sums


def target_rows(total, x_dev, z_dev, i_dev):
    pieces = [total[(i * 8 + x_dev * 2 + z_dev) * 8 : (i * 8 + x_dev * 2 + z_dev) * 8 + 8, :] for i in range(i_dev)]
    return jnp.concatenate(pieces, axis=0)


def own_z_kernel(z_ref, lam_ref, panel_ref, recv_ref, send_ref, keep_ref):
    i_dev = lam_ref.shape[0] // 64
    here = z_ref[0]
    sums = own_sum(lam_ref, panel_ref, recv_ref)
    levels = []
    size = 4 * i_dev * 8
    for block, total in enumerate(sums):
        low = jnp.concatenate([target_rows(total, x, 0, i_dev) for x in range(4)], axis=0)
        high = jnp.concatenate([target_rows(total, x, 1, i_dev) for x in range(4)], axis=0)
        keep_ref[0, block] = jnp.where(here == 0, low, high)
        code, level = encode(jnp.where(here == 0, high, low))
        send_ref[0, block * size : (block + 1) * size, :] = code
        levels.append(level)
    send_ref[0, len(sums) * size :, :] = level_rows(levels)


def own_z_part(z_dev, lam_rows, panel, recv, first, width):
    rows, depth = lam_rows.shape
    tiles, offset = width // TILE, first // TILE
    blocks = TILE // LANES
    size = blocks * (rows // 2) + SCALE_ROWS
    return pl.pallas_call(
        own_z_kernel,
        grid=(tiles,),
        in_specs=[
            pl.BlockSpec(memory_space=pltpu.SMEM),
            pl.BlockSpec((rows, depth), lambda t: (0, 0)),
            pl.BlockSpec((depth, TILE), lambda t: (0, t + offset)),
            pl.BlockSpec((1,) + recv.shape[1:], lambda t: (t, 0, 0)),
        ],
        out_specs=[
            pl.BlockSpec((1, size, LANES), lambda t: (t, 0, 0)),
            pl.BlockSpec((1, blocks, rows // 2, LANES), lambda t: (t, 0, 0, 0)),
        ],
        out_shape=[
            jax.ShapeDtypeStruct((tiles, size, LANES), jnp.int16),
            jax.ShapeDtypeStruct((tiles, blocks, rows // 2, LANES), jnp.float32),
        ],
        compiler_params=params(),
        cost_estimate=cost(rows, depth, width),
        name="own_z_part",
    )(z_dev, lam_rows, panel, recv)


def own_x_kernel(lam_ref, panel_ref, recv_ref, send_ref):
    i_dev = lam_ref.shape[0] // 64
    sums = own_sum(lam_ref, panel_ref, recv_ref)
    size = 2 * i_dev * 8
    for x in range(4):
        levels = []
        for block, total in enumerate(sums):
            rows = jnp.concatenate([target_rows(total, x, z, i_dev) for z in range(2)], axis=0)
            code, level = encode(rows)
            send_ref[x, 0, block * size : (block + 1) * size, :] = code
            levels.append(level)
        send_ref[x, 0, len(sums) * size :, :] = level_rows(levels)


def own_x_part(lam_rows, panel, recv, first, width):
    rows, depth = lam_rows.shape
    tiles, offset = width // TILE, first // TILE
    blocks = TILE // LANES
    size = blocks * (rows // 4) + SCALE_ROWS
    return pl.pallas_call(
        own_x_kernel,
        grid=(tiles,),
        in_specs=[
            pl.BlockSpec((rows, depth), lambda t: (0, 0)),
            pl.BlockSpec((depth, TILE), lambda t: (0, t + offset)),
            pl.BlockSpec((1,) + recv.shape[1:], lambda t: (t, 0, 0)),
        ],
        out_specs=pl.BlockSpec((4, 1, size, LANES), lambda t: (0, t, 0, 0)),
        out_shape=jax.ShapeDtypeStruct((4, tiles, size, LANES), jnp.int16),
        compiler_params=params(),
        cost_estimate=cost(rows, depth, width),
        name="own_x_part",
    )(lam_rows, panel, recv)


def merge_z_kernel(keep_ref, recv_ref, send_ref):
    tiles, blocks, rows, _ = keep_ref.shape
    owner = rows // 4
    levels = [[] for _ in range(4)]
    for tile in range(tiles):
        got = read_levels(recv_ref[tile, blocks * rows :, :])
        for block in range(blocks):
            at = (tile * blocks + block) * owner
            for x in range(4):
                part = slice(block * rows + x * owner, block * rows + (x + 1) * owner)
                total = keep_ref[tile, block, x * owner : (x + 1) * owner, :] + decode(
                    recv_ref[tile, part, :], got[block : block + 1, :]
                )
                code, level = encode(total)
                send_ref[x, at : at + owner, :] = code
                levels[x].append(level)
    for x in range(4):
        send_ref[x, tiles * blocks * owner :, :] = level_rows(levels[x])


def merge_z(keep, recv):
    tiles, blocks, rows, _ = keep.shape
    size = tiles * blocks * (rows // 4) + SCALE_ROWS
    return pl.pallas_call(
        merge_z_kernel,
        out_shape=jax.ShapeDtypeStruct((4, size, LANES), jnp.int16),
        compiler_params=params(),
        cost_estimate=cost(0, 0, 0, 6 * keep.size + 2 * recv.size),
        name="merge_z",
    )(keep, recv)


def merge_x_kernel(z_ref, recv_ref, send_ref, keep_ref):
    sources, tiles, size, _ = recv_ref.shape
    blocks = TILE // LANES
    rows = (size - SCALE_ROWS) // blocks
    owner = rows // 2
    here = z_ref[0]
    levels = []
    for tile in range(tiles):
        got = [read_levels(recv_ref[s, tile, blocks * rows :, :]) for s in range(sources)]
        for block in range(blocks):
            at = tile * blocks + block
            total = sum(
                decode(recv_ref[s, tile, block * rows : (block + 1) * rows, :], got[s][block : block + 1, :])
                for s in range(sources)
            )
            low, high = total[:owner, :], total[owner:, :]
            keep_ref[at] = jnp.where(here == 0, low, high)
            code, level = encode(jnp.where(here == 0, high, low))
            send_ref[at * owner : (at + 1) * owner, :] = code
            levels.append(level)
    send_ref[tiles * blocks * owner :, :] = level_rows(levels)


def merge_x(z_dev, recv):
    sources, tiles, size, _ = recv.shape
    blocks = TILE // LANES
    owner = (size - SCALE_ROWS) // blocks // 2
    return pl.pallas_call(
        merge_x_kernel,
        in_specs=[pl.BlockSpec(memory_space=pltpu.SMEM), pl.BlockSpec(memory_space=pltpu.VMEM)],
        out_shape=[
            jax.ShapeDtypeStruct((tiles * blocks * owner + SCALE_ROWS, LANES), jnp.int16),
            jax.ShapeDtypeStruct((tiles * blocks, owner, LANES), jnp.float32),
        ],
        compiler_params=params(),
        cost_estimate=cost(0, 0, 0, 2 * recv.size),
        name="merge_x",
    )(z_dev, recv)


def finish_kernel(z_recv_ref, x_keep_ref, x_recv_ref, cycle_ref, out_ref):
    sources = z_recv_ref.shape[0]
    x_blocks, rows, _ = x_keep_ref.shape
    z_blocks = (z_recv_ref.shape[1] - SCALE_ROWS) // rows
    i_dev = rows // 8
    z_levels = [read_levels(z_recv_ref[s, z_blocks * rows :, :]) for s in range(sources)]
    x_levels = read_levels(x_recv_ref[x_blocks * rows :, :])
    halves = BW // LANES

    def ladder(block):
        if block < z_blocks:
            part = slice(block * rows, (block + 1) * rows)
            return sum(decode(z_recv_ref[s, part, :], z_levels[s][block : block + 1, :]) for s in range(sources))
        block -= z_blocks
        part = slice(block * rows, (block + 1) * rows)
        return x_keep_ref[block] + decode(x_recv_ref[part, :], x_levels[block : block + 1, :])

    for half in range(halves):
        for group in range(AW // 8):
            totals = [ladder((group * 8 + a) * halves + half) for a in range(8)]
            for i in range(i_dev):
                stack = jnp.stack([total[i * 8 : (i + 1) * 8, :] for total in totals], axis=0)
                turned = jnp.swapaxes(stack, 0, 1)
                at = pl.ds(i * AW + group * 8, 8)
                for jj in range(8):
                    lanes = pl.ds(jj * BW + half * LANES, LANES)
                    out_ref[at, lanes] = turned[jj] + cycle_ref[at, lanes]


def finish(z_recv, x_keep, x_recv, cycle):
    return pl.pallas_call(
        finish_kernel,
        out_shape=jax.ShapeDtypeStruct(cycle.shape, jnp.float32),
        compiler_params=params(),
        cost_estimate=cost(0, 0, 0, 2 * z_recv.size + 6 * x_keep.size + 8 * cycle.size),
        name="finish",
    )(z_recv, x_keep, x_recv, cycle)


def cycle_kernel(kc_ref, jb_ref, amp_ref, packed_ref, spread_ref, out_ref):
    depth = packed_ref.shape[0]
    step = depth // 5
    total = jnp.zeros(out_ref.shape, jnp.float32)
    for part in range(5):
        rows = pl.ds(part * step, step)
        wide = jnp.dot(packed_ref[rows, :], spread_ref[...], preferred_element_type=jnp.float32)
        allowed = kc_ref[rows, :] == jb_ref[...]
        masked = jnp.where(allowed, wide, 0.0).astype(jnp.bfloat16)
        total += jnp.dot(amp_ref[:, part * step : (part + 1) * step], masked, preferred_element_type=jnp.float32)
    out_ref[...] = total


def cycle_term(kc_irrep, jb_irrep, amp, packed, spread):
    rows, depth = amp.shape
    pairs = packed.shape[1] // LANES
    width = spread.shape[1]
    return pl.pallas_call(
        cycle_kernel,
        grid=(pairs,),
        in_specs=[
            pl.BlockSpec((depth, 1), lambda t: (0, 0)),
            pl.BlockSpec((1, width), lambda t: (0, t)),
            pl.BlockSpec((rows, depth), lambda t: (0, 0)),
            pl.BlockSpec((depth, LANES), lambda t: (0, t)),
            pl.BlockSpec((LANES, width), lambda t: (0, 0)),
        ],
        out_specs=pl.BlockSpec((rows, width), lambda t: (0, t)),
        out_shape=jax.ShapeDtypeStruct((rows, pairs * width), jnp.float32),
        compiler_params=params(),
        cost_estimate=cost(2 * rows, depth, pairs * width),
        name="cycle_term",
    )(kc_irrep[:, None], jb_irrep[None, :], amp, packed, spread)


def swap(value, axis):
    return lax.ppermute(value, axis, [(0, 1), (1, 0)])


def labels_of(occ_irrep, virt_irrep):
    vir_count = lax.axis_size(VIR)
    j_width = JW // vir_count
    j_irrep = lax.dynamic_slice_in_dim(occ_irrep, lax.axis_index(VIR) * j_width, j_width, 0)
    jb_irrep = (j_irrep[:, None] ^ virt_irrep[None, :]).reshape(-1)
    kc_irrep = (occ_irrep[:, None] ^ virt_irrep[None, :PAN]).reshape(-1)
    return kc_irrep, jb_irrep


def device_step(packed_path, lam, ladder_int, cycle_amp, cycle_int, occ_irrep, virt_irrep):
    kc_irrep, jb_irrep = labels_of(occ_irrep, virt_irrep)
    if packed_path:
        mine = lax.dynamic_slice_in_dim(kc_irrep, lax.axis_index(OCC) * cycle_int.shape[0], cycle_int.shape[0], 0)
        place = jnp.arange(BW) - jnp.sum(virt_irrep[None, :] < virt_irrep[:, None], axis=1)
        one_hot = (jnp.arange(SEGMENT)[:, None] == place[None, :]).astype(jnp.bfloat16)
        group = LANES // SEGMENT
        spread = jnp.kron(jnp.eye(group, dtype=jnp.bfloat16), one_hot)
        masked = jnp.where(mine[:, None] == jb_irrep[None, :], cycle_int, jnp.zeros((), cycle_int.dtype))
        masked = masked.reshape(-1, group * BW)
        packed = jnp.dot(masked, spread.T, preferred_element_type=jnp.float32).astype(jnp.bfloat16)
        packed = packed.reshape(cycle_int.shape[0], -1)
        gathered = lax.all_gather(packed, OCC, axis=0, tiled=True)
    else:
        gathered = lax.all_gather(cycle_int, OCC, axis=0, tiled=True)

    rows, depth = lam.shape
    halves = lam.reshape(rows // 16, 2, 8, depth)
    core = lax.axis_index("core")
    z_dev = lax.axis_index("z_hi").astype(jnp.int32).reshape(1)
    other = lax.dynamic_index_in_dim(halves, 1 - core, 1, keepdims=False).reshape(rows // 2, depth)
    own = lax.dynamic_index_in_dim(halves, core, 1, keepdims=False).reshape(rows // 2, depth)
    columns = ladder_int.shape[1]
    x_columns = columns - Z_COLUMNS

    z_swapped = swap(partner_part(other, ladder_int, 0, Z_COLUMNS), "core")
    x_swapped = swap(partner_part(other, ladder_int, Z_COLUMNS, x_columns), "core")
    z_send, z_keep = own_z_part(z_dev, own, ladder_int, z_swapped, 0, Z_COLUMNS)
    z_recv = swap(z_send, "z_hi")
    x_send = own_x_part(own, ladder_int, x_swapped, Z_COLUMNS, x_columns)
    x_recv = lax.all_to_all(x_send, "x", 0, 0)
    z_second = lax.all_to_all(merge_z(z_keep, z_recv), "x", 0, 0)
    x_second_send, x_keep = merge_x(z_dev, x_recv)
    x_second = swap(x_second_send, "z_hi")

    if packed_path:
        cycle = cycle_term(kc_irrep, jb_irrep, cycle_amp, gathered, spread)
    else:
        allowed = kc_irrep[:, None] == jb_irrep[None, :]
        masked = jnp.where(allowed, gathered, jnp.zeros((), gathered.dtype))
        cycle = jnp.dot(cycle_amp, masked, preferred_element_type=jnp.float32)
    return finish(z_second, x_keep, x_second, cycle)


def per_device(lam, ladder_int, cycle_amp, cycle_int, occ_irrep, virt_irrep):
    longest = jnp.max(jnp.sum(virt_irrep[:, None] == jnp.arange(8)[None, :], axis=0))
    return lax.cond(
        longest <= SEGMENT,
        functools.partial(device_step, True),
        functools.partial(device_step, False),
        lam,
        ladder_int,
        cycle_amp,
        cycle_int,
        occ_irrep,
        virt_irrep,
    )


def solution(mesh):
    fine = Mesh(mesh.devices.reshape(2, 4, 4, 2, 2), ("z_lo", "y", "x", "z_hi", "core"))
    return jax.shard_map(
        per_device,
        mesh=fine,
        in_specs=(P(OCC, VIR), P(VIR, None), P(OCC, None), P(OCC, VIR), P(), P()),
        out_specs=P(OCC, VIR),
        check_vma=False,
    )
```

```python
import functools

import jax
import jax.numpy as jnp
from jax import lax
from jax.experimental import pallas as pl
from jax.experimental.pallas import tpu as pltpu
from jax.sharding import Mesh, PartitionSpec as P

PAN = 16
AW = 16
BW = 256
JW = 128
LANES = 128
HALVES = BW // LANES
SCALE_ROWS = 16
SEGMENT = 64
MIB = 1024 * 1024

VIR = ("x", "z_hi", "core")
OCC = ("z_lo", "y")
CHUNKS = (("x", 10, 5), ("z", 6, 2))
ORDER = ("P0", "P1", "O0", "O1", "C", "M0", "M1")
SCALE = 8


def encode(block):
    top = jnp.maximum(jnp.max(jnp.abs(block), axis=0, keepdims=True), 1e-30)
    level = jnp.ceil(jnp.log2(top) * 256.0) + 1.0
    step = jnp.exp2(level * (-1.0 / 256.0)) * 32767.0
    return jnp.round(block * step).astype(jnp.int32).astype(jnp.int16), level


def lane_block(value, block):
    return value[:, block * LANES : (block + 1) * LANES]


def decode(code, step):
    return code.astype(jnp.int32).astype(jnp.float32) * step


def level_rows(level):
    blocks = level.shape[1] // LANES
    rows = [lane_block(level, block) for block in range(blocks)]
    spare = jnp.zeros((1, LANES), jnp.float32)
    rows = jnp.concatenate(rows + [spare] * (SCALE_ROWS - blocks), axis=0)
    return rows.astype(jnp.int32).astype(jnp.int16)


def read_steps(block):
    level = block.astype(jnp.int32).astype(jnp.float32)
    return jnp.exp2(level * (1.0 / 256.0)) * (1.0 / 32767.0)


def params(mib):
    return pltpu.CompilerParams(vmem_limit_bytes=mib * MIB)


def in_hbm(value):
    return pltpu.with_memory_space_constraint(value, pltpu.HBM)


def in_vmem(value):
    return pltpu.with_memory_space_constraint(value, pltpu.VMEM)


def cost(rows, depth, columns, more=0):
    flops, moved = 2 * rows * depth * columns, 2 * (rows * depth + depth * columns) + more
    return pl.CostEstimate(flops=flops // SCALE, bytes_accessed=moved // SCALE + 1, transcendentals=0)


ANYWHERE = pl.BlockSpec(memory_space=pl.ANY)
SCALARS = pl.BlockSpec(memory_space=pltpu.SMEM)
WHOLE = pl.BlockSpec(memory_space=pltpu.VMEM)


def product(lam_rows, panel_ref):
    return jnp.dot(lam_rows, panel_ref[...], preferred_element_type=jnp.float32)


def partner_body(lam_rows, panel_ref, out_ref):
    rows = lam_rows.shape[0]
    acc = product(lam_rows, panel_ref)
    blocks = acc.shape[1] // LANES
    code, level = encode(acc)
    for block in range(blocks):
        out_ref[0, block * rows : (block + 1) * rows, :] = lane_block(code, block)
    out_ref[0, blocks * rows :, :] = level_rows(level)


def first_partner_kernel(lam_ref, panel_ref, _, out_ref, own_ref, other_ref):
    @pl.when(pl.program_id(0) == 0)
    def _select():
        here = lax.axis_index("core")
        for part in range(lam_ref.shape[0] // 32):
            rows = lam_ref[part * 32 : (part + 1) * 32, :].astype(jnp.float32)
            low = jnp.concatenate([rows[0:8], rows[16:24]], axis=0)
            high = jnp.concatenate([rows[8:16], rows[24:32]], axis=0)
            at = slice(part * 16, (part + 1) * 16)
            own_ref[at, :] = jnp.where(here == 0, low, high).astype(jnp.bfloat16)
            other_ref[at, :] = jnp.where(here == 0, high, low).astype(jnp.bfloat16)

    partner_body(other_ref[...], panel_ref, out_ref)


def first_partner_part(lam, panel, first, width, tile, after):
    rows, depth = lam.shape
    half = rows // 2
    tiles, offset = width // tile, first // tile
    size = tile // LANES * half + SCALE_ROWS
    return pl.pallas_call(
        first_partner_kernel,
        grid=(tiles,),
        in_specs=[
            pl.BlockSpec((rows, depth), lambda t: (0, 0)),
            pl.BlockSpec((depth, tile), lambda t: (0, t + offset)),
            ANYWHERE,
        ],
        out_specs=[
            pl.BlockSpec((1, size, LANES), lambda t: (t, 0, 0)),
            WHOLE,
            WHOLE,
        ],
        out_shape=[
            jax.ShapeDtypeStruct((tiles, size, LANES), jnp.int16),
            pltpu.VMEM((half, depth), jnp.bfloat16),
            pltpu.VMEM((half, depth), jnp.bfloat16),
        ],
        compiler_params=params(36),
        cost_estimate=cost(half, depth, width),
        name="partner_part",
    )(in_hbm(lam), in_hbm(panel), after)


def partner_kernel(lam_ref, panel_ref, _, out_ref):
    partner_body(lam_ref[...], panel_ref, out_ref)


def partner_part(lam_rows, panel, first, width, tile, after):
    rows, depth = lam_rows.shape
    tiles, offset = width // tile, first // tile
    size = tile // LANES * rows + SCALE_ROWS
    return pl.pallas_call(
        partner_kernel,
        grid=(tiles,),
        in_specs=[
            WHOLE,
            pl.BlockSpec((depth, tile), lambda t: (0, t + offset)),
            ANYWHERE,
        ],
        out_specs=pl.BlockSpec((1, size, LANES), lambda t: (t, 0, 0)),
        out_shape=jax.ShapeDtypeStruct((tiles, size, LANES), jnp.int16),
        compiler_params=params(20),
        cost_estimate=cost(rows, depth, width),
        name="partner_part",
    )(in_vmem(lam_rows), panel, after)


def own_sum(lam_ref, panel_ref, recv_ref):
    rows = lam_ref.shape[0]
    acc = product(lam_ref[...], panel_ref)
    blocks = acc.shape[1] // LANES
    tile = pl.program_id(0)
    steps = read_steps(recv_ref[tile, blocks * rows :, :])
    got = [
        decode(recv_ref[tile, block * rows : (block + 1) * rows, :], steps[block : block + 1, :])
        for block in range(blocks)
    ]
    return acc + jnp.concatenate(got, axis=1)


def target_rows(total, x_dev, z_dev, i_dev):
    pieces = [total[(i * 8 + x_dev * 2 + z_dev) * 8 : (i * 8 + x_dev * 2 + z_dev) * 8 + 8, :] for i in range(i_dev)]
    return jnp.concatenate(pieces, axis=0)


def own_z_kernel(lam_ref, panel_ref, recv_ref, _, send_ref, keep_ref):
    i_dev = lam_ref.shape[0] // 64
    here = lax.axis_index("z_hi")
    total = own_sum(lam_ref, panel_ref, recv_ref)
    blocks = total.shape[1] // LANES
    size = 4 * i_dev * 8
    low = jnp.concatenate([target_rows(total, x, 0, i_dev) for x in range(4)], axis=0)
    high = jnp.concatenate([target_rows(total, x, 1, i_dev) for x in range(4)], axis=0)
    keep = jnp.where(here == 0, low, high)
    code, level = encode(jnp.where(here == 0, high, low))
    for block in range(blocks):
        keep_ref[0, block] = lane_block(keep, block)
        send_ref[0, block * size : (block + 1) * size, :] = lane_block(code, block)
    send_ref[0, blocks * size :, :] = level_rows(level)


def own_z_part(lam_rows, panel, recv, first, width, tile, after):
    rows, depth = lam_rows.shape
    tiles, offset = width // tile, first // tile
    blocks = tile // LANES
    size = blocks * (rows // 2) + SCALE_ROWS
    return pl.pallas_call(
        own_z_kernel,
        grid=(tiles,),
        in_specs=[
            pl.BlockSpec((rows, depth), lambda t: (0, 0)),
            pl.BlockSpec((depth, tile), lambda t: (0, t + offset)),
            WHOLE,
            ANYWHERE,
        ],
        out_specs=[
            pl.BlockSpec((1, size, LANES), lambda t: (t, 0, 0)),
            pl.BlockSpec((1, blocks, rows // 2, LANES), lambda t: (t, 0, 0, 0)),
        ],
        out_shape=[
            jax.ShapeDtypeStruct((tiles, size, LANES), jnp.int16),
            pltpu.HBM((tiles, blocks, rows // 2, LANES), jnp.float32),
        ],
        compiler_params=params(26),
        cost_estimate=cost(rows, depth, width),
        name="own_z_part",
    )(in_hbm(lam_rows), in_hbm(panel), recv, after)


def own_x_kernel(lam_ref, panel_ref, recv_ref, _, send_ref):
    i_dev = lam_ref.shape[0] // 64
    total = own_sum(lam_ref, panel_ref, recv_ref)
    blocks = total.shape[1] // LANES
    size = 2 * i_dev * 8
    for x in range(4):
        code, level = encode(jnp.concatenate([target_rows(total, x, z, i_dev) for z in range(2)], axis=0))
        for block in range(blocks):
            send_ref[x, 0, block * size : (block + 1) * size, :] = lane_block(code, block)
        send_ref[x, 0, blocks * size :, :] = level_rows(level)


def own_x_part(lam_rows, panel, recv, first, width, tile, after):
    rows, depth = lam_rows.shape
    tiles, offset = width // tile, first // tile
    blocks = tile // LANES
    size = blocks * (rows // 4) + SCALE_ROWS
    return pl.pallas_call(
        own_x_kernel,
        grid=(tiles,),
        in_specs=[
            WHOLE,
            pl.BlockSpec((depth, tile), lambda t: (0, t + offset)),
            WHOLE,
            ANYWHERE,
        ],
        out_specs=pl.BlockSpec((4, 1, size, LANES), lambda t: (0, t, 0, 0)),
        out_shape=jax.ShapeDtypeStruct((4, tiles, size, LANES), jnp.int16),
        compiler_params=params(26),
        cost_estimate=cost(rows, depth, width),
        name="own_x_part",
    )(in_vmem(lam_rows), in_hbm(panel), recv, after)


def merge_z_kernel(keep_ref, recv_ref, _, send_ref):
    blocks, rows = keep_ref.shape[1:3]
    owner = rows // 4
    tile = pl.program_id(0)
    steps = read_steps(recv_ref[tile, blocks * rows :, :])
    totals = []
    for x in range(4):
        for block in range(blocks):
            part = slice(block * rows + x * owner, block * rows + (x + 1) * owner)
            got = decode(recv_ref[tile, part, :], steps[block : block + 1, :])
            totals.append(keep_ref[0, block, x * owner : (x + 1) * owner, :] + got)
    code, level = encode(jnp.concatenate(totals, axis=1))
    for x in range(4):
        for block in range(blocks):
            send_ref[x, 0, block * owner : (block + 1) * owner, :] = lane_block(code, x * blocks + block)
        mine = slice(x * blocks * LANES, (x + 1) * blocks * LANES)
        send_ref[x, 0, blocks * owner :, :] = level_rows(level[:, mine])


def merge_z(keep, recv, after):
    tiles, blocks, rows, _ = keep.shape
    size = blocks * (rows // 4) + SCALE_ROWS
    return pl.pallas_call(
        merge_z_kernel,
        grid=(tiles,),
        in_specs=[
            pl.BlockSpec((1,) + keep.shape[1:], lambda t: (t, 0, 0, 0)),
            WHOLE,
            ANYWHERE,
        ],
        out_specs=pl.BlockSpec((4, 1, size, LANES), lambda t: (0, t, 0, 0)),
        out_shape=jax.ShapeDtypeStruct((4, tiles, size, LANES), jnp.int16),
        compiler_params=params(10),
        cost_estimate=cost(0, 0, 0, 6 * keep.size + 2 * recv.size),
        name="merge_z",
    )(in_hbm(keep), recv, after)


def merge_x_kernel(recv_ref, _, send_ref, keep_ref):
    sources = recv_ref.shape[0]
    tile = pl.program_id(0)
    blocks, owner = keep_ref.shape[1:3]
    rows = 2 * owner
    here = lax.axis_index("z_hi")
    steps = [read_steps(recv_ref[s, tile, blocks * rows :, :]) for s in range(sources)]
    sends = []
    for block in range(blocks):
        part = slice(block * rows, (block + 1) * rows)
        total = sum(decode(recv_ref[s, tile, part, :], steps[s][block : block + 1, :]) for s in range(sources))
        low, high = total[:owner, :], total[owner:, :]
        keep_ref[0, block] = jnp.where(here == 0, low, high)
        sends.append(jnp.where(here == 0, high, low))
    code, level = encode(jnp.concatenate(sends, axis=1))
    for block in range(blocks):
        send_ref[0, block * owner : (block + 1) * owner, :] = lane_block(code, block)
    send_ref[0, blocks * owner :, :] = level_rows(level)


def merge_x(recv, blocks, after):
    sources, tiles, size, _ = recv.shape
    owner = (size - SCALE_ROWS) // blocks // 2
    return pl.pallas_call(
        merge_x_kernel,
        grid=(tiles,),
        in_specs=[
            WHOLE,
            ANYWHERE,
        ],
        out_specs=[
            pl.BlockSpec((1, blocks * owner + SCALE_ROWS, LANES), lambda t: (t, 0, 0)),
            pl.BlockSpec((1, blocks, owner, LANES), lambda t: (t, 0, 0, 0)),
        ],
        out_shape=[
            pltpu.HBM((tiles, blocks * owner + SCALE_ROWS, LANES), jnp.int16),
            pltpu.HBM((tiles, blocks, owner, LANES), jnp.float32),
        ],
        compiler_params=params(10),
        cost_estimate=cost(0, 0, 0, 2 * recv.size),
        name="merge_x",
    )(recv, after)


def finish_kernel(*refs):
    cycle_ref, out_ref = refs[-2:]
    refs = refs[:-2]
    rows = JW // 16 * 8
    i_dev = rows // 8
    blocks = []
    for kind, _, tile_a in CHUNKS:
        count = tile_a * HALVES
        if kind == "z":
            recv_ref, refs = refs[0], refs[1:]
            sources, tiles = recv_ref.shape[:2]
            for tile in range(tiles):
                levels = [read_steps(recv_ref[s, tile, count * rows :, :]) for s in range(sources)]

                def summed(block, ref=recv_ref, tile=tile, levels=levels):
                    part = slice(block * rows, (block + 1) * rows)
                    return sum(
                        decode(ref[s, tile, part, :], levels[s][block : block + 1, :]) for s in range(len(levels))
                    )

                blocks += [functools.partial(summed, block) for block in range(count)]
        else:
            (keep_ref, recv_ref), refs = refs[:2], refs[2:]
            for tile in range(recv_ref.shape[0]):
                levels = read_steps(recv_ref[tile, count * rows :, :])

                def kept(block, keep=keep_ref, ref=recv_ref, tile=tile, levels=levels):
                    part = slice(block * rows, (block + 1) * rows)
                    return keep[tile, block] + decode(ref[tile, part, :], levels[block : block + 1, :])

                blocks += [functools.partial(kept, block) for block in range(count)]

    for group in range(AW // 8):

        @pl.when(pl.program_id(0) == group)
        def _group(group=group):
            for half in range(HALVES):
                totals = [blocks[(group * 8 + a) * HALVES + half]() for a in range(8)]
                for i in range(i_dev):
                    stack = jnp.stack([total[i * 8 : (i + 1) * 8, :] for total in totals], axis=0)
                    turned = jnp.swapaxes(stack, 0, 1)
                    for jj in range(8):
                        lanes = pl.ds(jj * BW + half * LANES, LANES)
                        out_ref[i, 0, :, lanes] = turned[jj] + cycle_ref[i, 0, :, lanes]


def finish(parts, cycle):
    rows, columns = cycle.shape
    shape = (rows // AW, AW // 8, 8, columns)
    block = pl.BlockSpec((shape[0], 1, 8, columns), lambda t: (0, t, 0, 0))
    out = pl.pallas_call(
        finish_kernel,
        grid=(AW // 8,),
        in_specs=[WHOLE] * len(parts) + [block],
        out_specs=block,
        out_shape=pltpu.HBM(shape, jnp.float32),
        compiler_params=params(12),
        cost_estimate=cost(0, 0, 0, 16 * cycle.size),
        name="finish",
    )(*[in_hbm(part) if part.dtype == jnp.float32 else in_vmem(part) for part in parts], cycle.reshape(shape))
    return out.reshape(rows, columns)


def one_hot_places(virt):
    start = jnp.zeros(virt.shape, jnp.int32)
    for label in range(8):
        below = jnp.sum((virt < label).astype(jnp.int32), axis=1, keepdims=True)
        start = jnp.where(virt == label, below, start)
    place = lax.broadcasted_iota(jnp.int32, virt.shape, 1) - start
    return lax.broadcasted_iota(jnp.int32, (SEGMENT, BW), 0) == place


def spread_matrix(virt):
    hot = one_hot_places(virt).astype(jnp.float32)
    none = jnp.zeros_like(hot)
    group = LANES // SEGMENT
    rows = [jnp.concatenate([hot if a == b else none for b in range(group)], axis=1) for a in range(group)]
    return jnp.concatenate(rows, axis=0).astype(jnp.bfloat16)


def row_labels(occ, virt, first, rows):
    row = lax.broadcasted_iota(jnp.int32, (rows, 1), 0)
    k = first + row // PAN
    lane = lax.broadcasted_iota(jnp.int32, (rows, occ.shape[1]), 1)
    k_label = jnp.sum(jnp.where(lane == k, occ, 0), axis=1, keepdims=True)
    lane = lax.broadcasted_iota(jnp.int32, (rows, LANES), 1)
    c_label = jnp.sum(jnp.where(lane == row % PAN, virt[:, :LANES], 0), axis=1, keepdims=True)
    return k_label ^ c_label


def pack_kernel(occ_s_ref, occ_ref, virt_ref, cycle_ref, packed_ref, jb_ref):
    rows, columns = cycle_ref.shape
    virt = virt_ref[...]
    mine = row_labels(occ_ref[...], virt, lax.axis_index(OCC) * (rows // PAN), rows)
    spread = spread_matrix(virt)
    width = spread.shape[1]
    for step in range(columns // width):
        lanes = slice(step * width, (step + 1) * width)
        first = (lax.axis_index(VIR) * (columns // width) + step) * (width // BW)
        jb = jnp.concatenate([virt ^ occ_s_ref[first + jj] for jj in range(width // BW)], axis=1)
        jb_ref[:, lanes] = jb
        masked = jnp.where(mine == jb, cycle_ref[:, lanes].astype(jnp.float32), 0.0).astype(jnp.bfloat16)
        packed_ref[:, step * LANES : (step + 1) * LANES] = lax.dot_general(
            masked, spread, (((1,), (1,)), ((), ())), preferred_element_type=jnp.float32
        ).astype(jnp.bfloat16)


def pack(occ_irrep, virt_irrep, cycle_int):
    rows, columns = cycle_int.shape
    width = columns * SEGMENT // BW
    return pl.pallas_call(
        pack_kernel,
        in_specs=[SCALARS, WHOLE, WHOLE, WHOLE],
        out_shape=[
            jax.ShapeDtypeStruct((rows, width), jnp.bfloat16),
            jax.ShapeDtypeStruct((1, columns), jnp.int32),
        ],
        compiler_params=params(12),
        cost_estimate=cost(rows, LANES, columns),
        name="pack",
    )(occ_irrep, occ_irrep[None, :], virt_irrep[None, :], in_hbm(cycle_int))


def lane_labels(occ_s, virt_s, depth):
    lane = lax.broadcasted_iota(jnp.int32, (1, LANES), 1)
    c_label = jnp.zeros((1, LANES), jnp.int32)
    for c in range(PAN):
        c_label = jnp.where(lane % PAN == c, virt_s[c], c_label)
    pieces = []
    per_row = LANES // PAN
    for row in range(depth // LANES):
        k_label = jnp.zeros((1, LANES), jnp.int32)
        for m in range(per_row):
            k_label = jnp.where(lane // PAN == m, occ_s[row * per_row + m], k_label)
        pieces.append(k_label ^ c_label)
    return jnp.concatenate(pieces, axis=1)


def cycle_kernel(occ_s_ref, virt_s_ref, virt_ref, jb_ref, amp_ref, packed_ref, _, out_ref, split_ref):
    rows, depth = amp_ref.shape
    width = LANES // SEGMENT * BW

    @pl.when(pl.program_id(0) == 0)
    def _split():
        label = lane_labels(occ_s_ref, virt_s_ref, depth)
        amp = amp_ref[...].astype(jnp.float32)
        for g in range(8):
            split_ref[g * rows : (g + 1) * rows, :] = jnp.where(label == g, amp, 0.0).astype(jnp.bfloat16)

    parts = jnp.dot(split_ref[...], packed_ref[...], preferred_element_type=jnp.float32)
    spread = spread_matrix(virt_ref[...]).astype(jnp.float32)
    for pair in range(packed_ref.shape[1] // LANES):
        lanes = slice(pair * LANES, (pair + 1) * LANES)
        wide = jnp.concatenate([parts[g * rows : (g + 1) * rows, lanes] for g in range(8)], axis=1)
        high = wide.astype(jnp.bfloat16)
        low = (wide - high.astype(jnp.float32)).astype(jnp.bfloat16)
        jb = jb_ref[:, pair * width : (pair + 1) * width]
        choose = jnp.concatenate([jnp.where(jb == g, spread, 0.0).astype(jnp.bfloat16) for g in range(8)], axis=0)
        both = jnp.dot(jnp.concatenate([high, low], axis=0), choose, preferred_element_type=jnp.float32)
        out_ref[:, pair * width : (pair + 1) * width] = both[:rows, :] + both[rows:, :]


def cycle_term(occ_irrep, virt_irrep, jb_irrep, amp, packed, after):
    rows, depth = amp.shape
    steps = 2
    columns = jb_irrep.shape[1]
    return pl.pallas_call(
        cycle_kernel,
        grid=(steps,),
        in_specs=[
            SCALARS,
            SCALARS,
            WHOLE,
            pl.BlockSpec((1, columns // steps), lambda t: (0, t)),
            pl.BlockSpec((rows, depth), lambda t: (0, 0)),
            pl.BlockSpec((depth, packed.shape[1] // steps), lambda t: (0, t)),
            ANYWHERE,
        ],
        out_specs=pl.BlockSpec((rows, columns // steps), lambda t: (0, t)),
        out_shape=jax.ShapeDtypeStruct((rows, columns), jnp.float32),
        scratch_shapes=[pltpu.VMEM((8 * rows, depth), jnp.bfloat16)],
        compiler_params=params(28),
        cost_estimate=cost(2 * rows, depth, columns),
        name="cycle_term",
    )(in_hbm(occ_irrep), in_hbm(virt_irrep), virt_irrep[None, :], jb_irrep, in_hbm(amp), in_hbm(packed), after)


def swap(value, axis):
    return lax.ppermute(value, axis, [(0, 1), (1, 0)])


def exchange(value):
    return lax.all_to_all(value, "x", 0, 0)


def dense_cycle(amp, cycle_int, occ_irrep, virt_irrep, j_first, j_width):
    gathered = lax.all_gather(cycle_int, OCC, axis=0, tiled=True)
    kc_irrep = (occ_irrep[:, None] ^ virt_irrep[None, :PAN]).reshape(-1)
    jb_irrep = lax.dynamic_slice_in_dim(occ_irrep, j_first, j_width, 0)[:, None] ^ virt_irrep[None, :]
    allowed = kc_irrep[:, None] == jb_irrep.reshape(1, -1)
    masked = jnp.where(allowed, gathered, jnp.zeros((), gathered.dtype))
    return jnp.dot(amp, masked, preferred_element_type=jnp.float32)


def per_device(lam, ladder_int, cycle_amp, cycle_int, occ_irrep, virt_irrep):
    j_width = JW // lax.axis_size(VIR)
    j_first = lax.axis_index(VIR) * j_width
    fits = jnp.all(virt_irrep[SEGMENT:] != virt_irrep[:-SEGMENT])
    last, jb_irrep = pack(occ_irrep, virt_irrep, cycle_int)
    gathered = lax.all_gather(last, OCC, axis=0, tiled=True)

    kinds = [kind for kind, _, _ in CHUNKS]
    widths = [a * BW for _, a, _ in CHUNKS]
    tiles = [a * BW for _, _, a in CHUNKS]
    firsts = [sum(widths[:n]) for n in range(len(CHUNKS))]
    lam_rows = {}
    core_got, sent, kept, second = {}, {}, {}, {}

    def partner(n, last):
        if not lam_rows:
            last, lam_rows["own"], lam_rows["other"] = first_partner_part(
                lam, ladder_int, firsts[n], widths[n], tiles[n], last
            )
        else:
            last = partner_part(lam_rows["other"], ladder_int, firsts[n], widths[n], tiles[n], last)
        core_got[n] = swap(last, "core")
        return last

    def own(n, last):
        args = (lam_rows["own"], ladder_int, core_got[n], firsts[n], widths[n], tiles[n], last)
        if kinds[n] == "z":
            last, kept[n] = own_z_part(*args)
            sent[n] = swap(last, "z_hi")
        else:
            last = own_x_part(*args)
            sent[n] = exchange(last)
        return last

    def merge(n, last):
        if kinds[n] == "z":
            last = merge_z(kept[n], sent[n], last)
            second[n] = [exchange(last)]
        else:
            last, keep = merge_x(sent[n], tiles[n] // LANES, last)
            second[n] = [keep, swap(last, "z_hi")]
        return last

    for step in ORDER:
        if step == "C":
            cycle = lax.cond(
                fits,
                lambda gathered, jb, amp, own, occ, virt, last: cycle_term(occ, virt, jb, amp, gathered, last),
                lambda gathered, jb, amp, own, occ, virt, last: dense_cycle(amp, own, occ, virt, j_first, j_width),
                *(gathered, jb_irrep, cycle_amp, cycle_int, occ_irrep, virt_irrep, last),
            )
            last = cycle
        else:
            last = {"P": partner, "O": own, "M": merge}[step[0]](int(step[1]), last)
    return finish([part for n in range(len(CHUNKS)) for part in second[n]], cycle)


def solution(mesh):
    fine = Mesh(mesh.devices.reshape(2, 4, 4, 2, 2), ("z_lo", "y", "x", "z_hi", "core"))
    return jax.shard_map(
        per_device,
        mesh=fine,
        in_specs=(P(OCC, VIR), P(VIR, None), P(OCC, None), P(OCC, VIR), P(), P()),
        out_specs=P(OCC, VIR),
        check_vma=False,
    )
```

```python
import functools

import jax
import jax.numpy as jnp
from jax import lax
from jax.experimental import pallas as pl
from jax.experimental.pallas import tpu as pltpu
from jax.sharding import Mesh, PartitionSpec as P

PAN = 16
AW = 16
BW = 256
JW = 128
LANES = 128
HALVES = BW // LANES
SCALE_ROWS = 16
SEGMENT = 64
MIB = 1024 * 1024

VIR = ("x", "z_hi", "core")
OCC = ("z_lo", "y")
CHUNKS = (("x", 10, 5), ("z", 6, 2))
ORDER = ("P0", "P1", "O0", "O1", "C", "M0", "M1")
SCALE = 8


def encode(block):
    top = jnp.maximum(jnp.max(jnp.abs(block), axis=0, keepdims=True), 1e-30)
    level = jnp.ceil(jnp.log2(top) * 256.0) + 1.0
    step = jnp.exp2(level * (-1.0 / 256.0)) * 32767.0
    return jnp.round(block * step).astype(jnp.int32).astype(jnp.int16), level


def lane_block(value, block):
    return value[:, block * LANES : (block + 1) * LANES]


def decode(code, step):
    return code.astype(jnp.int32).astype(jnp.float32) * step


def level_rows(level):
    blocks = level.shape[1] // LANES
    rows = [lane_block(level, block) for block in range(blocks)]
    spare = jnp.zeros((1, LANES), jnp.float32)
    rows = jnp.concatenate(rows + [spare] * (SCALE_ROWS - blocks), axis=0)
    return rows.astype(jnp.int32).astype(jnp.int16)


def read_steps(block):
    level = block.astype(jnp.int32).astype(jnp.float32)
    return jnp.exp2(level * (1.0 / 256.0)) * (1.0 / 32767.0)


def params(mib):
    return pltpu.CompilerParams(vmem_limit_bytes=mib * MIB)


def in_hbm(value):
    return pltpu.with_memory_space_constraint(value, pltpu.HBM)


def in_vmem(value):
    return pltpu.with_memory_space_constraint(value, pltpu.VMEM)


def cost(rows, depth, columns, more=0):
    flops, moved = 2 * rows * depth * columns, 2 * (rows * depth + depth * columns) + more
    return pl.CostEstimate(flops=flops // SCALE, bytes_accessed=moved // SCALE + 1, transcendentals=0)


ANYWHERE = pl.BlockSpec(memory_space=pl.ANY)
SCALARS = pl.BlockSpec(memory_space=pltpu.SMEM)
WHOLE = pl.BlockSpec(memory_space=pltpu.VMEM)


def product(lam_rows, panel_ref):
    return jnp.dot(lam_rows, panel_ref[...], preferred_element_type=jnp.float32)


def partner_body(lam_rows, panel_ref, out_ref):
    rows = lam_rows.shape[0]
    acc = product(lam_rows, panel_ref)
    blocks = acc.shape[1] // LANES
    code, level = encode(acc)
    for block in range(blocks):
        out_ref[0, block * rows : (block + 1) * rows, :] = lane_block(code, block)
    out_ref[0, blocks * rows :, :] = level_rows(level)


def first_partner_kernel(lam_ref, panel_ref, _, out_ref, own_ref, other_ref):
    @pl.when(pl.program_id(0) == 0)
    def _select():
        here = lax.axis_index("core")
        for part in range(lam_ref.shape[0] // 32):
            rows = lam_ref[part * 32 : (part + 1) * 32, :].astype(jnp.float32)
            low = jnp.concatenate([rows[0:8], rows[16:24]], axis=0)
            high = jnp.concatenate([rows[8:16], rows[24:32]], axis=0)
            at = slice(part * 16, (part + 1) * 16)
            own_ref[at, :] = jnp.where(here == 0, low, high).astype(jnp.bfloat16)
            other_ref[at, :] = jnp.where(here == 0, high, low).astype(jnp.bfloat16)

    partner_body(other_ref[...], panel_ref, out_ref)


def first_partner_part(lam, panel, first, width, tile, after):
    rows, depth = lam.shape
    half = rows // 2
    tiles, offset = width // tile, first // tile
    size = tile // LANES * half + SCALE_ROWS
    return pl.pallas_call(
        first_partner_kernel,
        grid=(tiles,),
        in_specs=[
            pl.BlockSpec((rows, depth), lambda t: (0, 0)),
            pl.BlockSpec((depth, tile), lambda t: (0, t + offset)),
            ANYWHERE,
        ],
        out_specs=[
            pl.BlockSpec((1, size, LANES), lambda t: (t, 0, 0)),
            WHOLE,
            WHOLE,
        ],
        out_shape=[
            jax.ShapeDtypeStruct((tiles, size, LANES), jnp.int16),
            pltpu.VMEM((half, depth), jnp.bfloat16),
            pltpu.VMEM((half, depth), jnp.bfloat16),
        ],
        compiler_params=params(36),
        cost_estimate=cost(half, depth, width),
        name="partner_part",
    )(in_hbm(lam), in_hbm(panel), after)


def partner_kernel(lam_ref, panel_ref, _, out_ref):
    partner_body(lam_ref[...], panel_ref, out_ref)


def partner_part(lam_rows, panel, first, width, tile, after):
    rows, depth = lam_rows.shape
    tiles, offset = width // tile, first // tile
    size = tile // LANES * rows + SCALE_ROWS
    return pl.pallas_call(
        partner_kernel,
        grid=(tiles,),
        in_specs=[
            WHOLE,
            pl.BlockSpec((depth, tile), lambda t: (0, t + offset)),
            ANYWHERE,
        ],
        out_specs=pl.BlockSpec((1, size, LANES), lambda t: (t, 0, 0)),
        out_shape=jax.ShapeDtypeStruct((tiles, size, LANES), jnp.int16),
        compiler_params=params(20),
        cost_estimate=cost(rows, depth, width),
        name="partner_part",
    )(in_vmem(lam_rows), in_vmem(panel), after)


def own_sum(lam_ref, panel_ref, recv_ref):
    rows = lam_ref.shape[0]
    acc = product(lam_ref[...], panel_ref)
    blocks = acc.shape[1] // LANES
    tile = pl.program_id(0)
    steps = read_steps(recv_ref[tile, blocks * rows :, :])
    got = [
        decode(recv_ref[tile, block * rows : (block + 1) * rows, :], steps[block : block + 1, :])
        for block in range(blocks)
    ]
    return acc + jnp.concatenate(got, axis=1)


def target_rows(total, x_dev, z_dev, i_dev):
    pieces = [total[(i * 8 + x_dev * 2 + z_dev) * 8 : (i * 8 + x_dev * 2 + z_dev) * 8 + 8, :] for i in range(i_dev)]
    return jnp.concatenate(pieces, axis=0)


def own_z_kernel(lam_ref, panel_ref, recv_ref, _, send_ref, keep_ref):
    i_dev = lam_ref.shape[0] // 64
    here = lax.axis_index("z_hi")
    total = own_sum(lam_ref, panel_ref, recv_ref)
    blocks = total.shape[1] // LANES
    size = 4 * i_dev * 8
    low = jnp.concatenate([target_rows(total, x, 0, i_dev) for x in range(4)], axis=0)
    high = jnp.concatenate([target_rows(total, x, 1, i_dev) for x in range(4)], axis=0)
    keep = jnp.where(here == 0, low, high)
    code, level = encode(jnp.where(here == 0, high, low))
    for block in range(blocks):
        keep_ref[0, block] = lane_block(keep, block)
        send_ref[0, block * size : (block + 1) * size, :] = lane_block(code, block)
    send_ref[0, blocks * size :, :] = level_rows(level)


def own_z_part(lam_rows, panel, recv, first, width, tile, after):
    rows, depth = lam_rows.shape
    tiles, offset = width // tile, first // tile
    blocks = tile // LANES
    size = blocks * (rows // 2) + SCALE_ROWS
    return pl.pallas_call(
        own_z_kernel,
        grid=(tiles,),
        in_specs=[
            pl.BlockSpec((rows, depth), lambda t: (0, 0)),
            pl.BlockSpec((depth, tile), lambda t: (0, t + offset)),
            WHOLE,
            ANYWHERE,
        ],
        out_specs=[
            pl.BlockSpec((1, size, LANES), lambda t: (t, 0, 0)),
            pl.BlockSpec((1, blocks, rows // 2, LANES), lambda t: (t, 0, 0, 0)),
        ],
        out_shape=[
            jax.ShapeDtypeStruct((tiles, size, LANES), jnp.int16),
            pltpu.HBM((tiles, blocks, rows // 2, LANES), jnp.float32),
        ],
        compiler_params=params(26),
        cost_estimate=cost(rows, depth, width),
        name="own_z_part",
    )(in_hbm(lam_rows), in_hbm(panel), recv, after)


def own_x_kernel(lam_ref, panel_ref, recv_ref, _, send_ref):
    i_dev = lam_ref.shape[0] // 64
    total = own_sum(lam_ref, panel_ref, recv_ref)
    blocks = total.shape[1] // LANES
    size = 2 * i_dev * 8
    for x in range(4):
        code, level = encode(jnp.concatenate([target_rows(total, x, z, i_dev) for z in range(2)], axis=0))
        for block in range(blocks):
            send_ref[x, 0, block * size : (block + 1) * size, :] = lane_block(code, block)
        send_ref[x, 0, blocks * size :, :] = level_rows(level)


def own_x_part(lam_rows, panel, recv, first, width, tile, after):
    rows, depth = lam_rows.shape
    tiles, offset = width // tile, first // tile
    blocks = tile // LANES
    size = blocks * (rows // 4) + SCALE_ROWS
    return pl.pallas_call(
        own_x_kernel,
        grid=(tiles,),
        in_specs=[
            WHOLE,
            pl.BlockSpec((depth, tile), lambda t: (0, t + offset)),
            WHOLE,
            ANYWHERE,
        ],
        out_specs=pl.BlockSpec((4, 1, size, LANES), lambda t: (0, t, 0, 0)),
        out_shape=jax.ShapeDtypeStruct((4, tiles, size, LANES), jnp.int16),
        compiler_params=params(26),
        cost_estimate=cost(rows, depth, width),
        name="own_x_part",
    )(in_vmem(lam_rows), in_vmem(panel), recv, after)


def merge_z_kernel(keep_ref, recv_ref, _, send_ref):
    blocks, rows = keep_ref.shape[1:3]
    owner = rows // 4
    tile = pl.program_id(0)
    steps = read_steps(recv_ref[tile, blocks * rows :, :])
    totals = []
    for x in range(4):
        for block in range(blocks):
            part = slice(block * rows + x * owner, block * rows + (x + 1) * owner)
            got = decode(recv_ref[tile, part, :], steps[block : block + 1, :])
            totals.append(keep_ref[tile, block, x * owner : (x + 1) * owner, :] + got)
    code, level = encode(jnp.concatenate(totals, axis=1))
    for x in range(4):
        for block in range(blocks):
            send_ref[x, 0, block * owner : (block + 1) * owner, :] = lane_block(code, x * blocks + block)
        mine = slice(x * blocks * LANES, (x + 1) * blocks * LANES)
        send_ref[x, 0, blocks * owner :, :] = level_rows(level[:, mine])


def merge_z(keep, recv, after):
    tiles, blocks, rows, _ = keep.shape
    size = blocks * (rows // 4) + SCALE_ROWS
    return pl.pallas_call(
        merge_z_kernel,
        grid=(tiles,),
        in_specs=[
            WHOLE,
            WHOLE,
            ANYWHERE,
        ],
        out_specs=pl.BlockSpec((4, 1, size, LANES), lambda t: (0, t, 0, 0)),
        out_shape=jax.ShapeDtypeStruct((4, tiles, size, LANES), jnp.int16),
        compiler_params=params(10),
        cost_estimate=cost(0, 0, 0, 6 * keep.size + 2 * recv.size),
        name="merge_z",
    )(in_vmem(keep), recv, in_hbm(after))


def merge_x_kernel(recv_ref, _, send_ref, keep_ref):
    sources = recv_ref.shape[0]
    tile = pl.program_id(0)
    blocks, owner = keep_ref.shape[1:3]
    rows = 2 * owner
    here = lax.axis_index("z_hi")
    steps = [read_steps(recv_ref[s, tile, blocks * rows :, :]) for s in range(sources)]
    sends = []
    for block in range(blocks):
        part = slice(block * rows, (block + 1) * rows)
        total = sum(decode(recv_ref[s, tile, part, :], steps[s][block : block + 1, :]) for s in range(sources))
        low, high = total[:owner, :], total[owner:, :]
        keep_ref[0, block] = jnp.where(here == 0, low, high)
        sends.append(jnp.where(here == 0, high, low))
    code, level = encode(jnp.concatenate(sends, axis=1))
    for block in range(blocks):
        send_ref[0, block * owner : (block + 1) * owner, :] = lane_block(code, block)
    send_ref[0, blocks * owner :, :] = level_rows(level)


def merge_x(recv, blocks, after):
    sources, tiles, size, _ = recv.shape
    owner = (size - SCALE_ROWS) // blocks // 2
    return pl.pallas_call(
        merge_x_kernel,
        grid=(tiles,),
        in_specs=[
            WHOLE,
            ANYWHERE,
        ],
        out_specs=[
            pl.BlockSpec((1, blocks * owner + SCALE_ROWS, LANES), lambda t: (t, 0, 0)),
            pl.BlockSpec((1, blocks, owner, LANES), lambda t: (t, 0, 0, 0)),
        ],
        out_shape=[
            pltpu.HBM((tiles, blocks * owner + SCALE_ROWS, LANES), jnp.int16),
            pltpu.HBM((tiles, blocks, owner, LANES), jnp.float32),
        ],
        compiler_params=params(10),
        cost_estimate=cost(0, 0, 0, 2 * recv.size),
        name="merge_x",
    )(recv, after)


def finish_kernel(*refs):
    cycle_ref, out_ref = refs[-2:]
    refs = refs[:-2]
    rows = JW // 16 * 8
    i_dev = rows // 8
    blocks = []
    for kind, _, tile_a in CHUNKS:
        count = tile_a * HALVES
        if kind == "z":
            recv_ref, refs = refs[0], refs[1:]
            sources, tiles = recv_ref.shape[:2]
            for tile in range(tiles):
                levels = [read_steps(recv_ref[s, tile, count * rows :, :]) for s in range(sources)]

                def summed(block, ref=recv_ref, tile=tile, levels=levels):
                    part = slice(block * rows, (block + 1) * rows)
                    return sum(
                        decode(ref[s, tile, part, :], levels[s][block : block + 1, :]) for s in range(len(levels))
                    )

                blocks += [functools.partial(summed, block) for block in range(count)]
        else:
            (keep_ref, recv_ref), refs = refs[:2], refs[2:]
            for tile in range(recv_ref.shape[0]):
                levels = read_steps(recv_ref[tile, count * rows :, :])

                def kept(block, keep=keep_ref, ref=recv_ref, tile=tile, levels=levels):
                    part = slice(block * rows, (block + 1) * rows)
                    return keep[tile, block] + decode(ref[tile, part, :], levels[block : block + 1, :])

                blocks += [functools.partial(kept, block) for block in range(count)]

    for group in range(AW // 8):

        @pl.when(pl.program_id(0) == group)
        def _group(group=group):
            for half in range(HALVES):
                totals = [blocks[(group * 8 + a) * HALVES + half]() for a in range(8)]
                for i in range(i_dev):
                    stack = jnp.stack([total[i * 8 : (i + 1) * 8, :] for total in totals], axis=0)
                    turned = jnp.swapaxes(stack, 0, 1)
                    for jj in range(8):
                        lanes = pl.ds(jj * BW + half * LANES, LANES)
                        out_ref[i, 0, :, lanes] = turned[jj] + cycle_ref[i, 0, :, lanes]


def finish(parts, cycle):
    shape = cycle.shape
    columns = shape[-1]
    block = pl.BlockSpec((shape[0], 1, 8, columns), lambda t: (0, t, 0, 0))
    out = pl.pallas_call(
        finish_kernel,
        grid=(AW // 8,),
        in_specs=[WHOLE] * len(parts) + [block],
        out_specs=block,
        out_shape=pltpu.HBM(shape, jnp.float32),
        compiler_params=params(12),
        cost_estimate=cost(0, 0, 0, 16 * cycle.size),
        name="finish",
    )(*[in_hbm(part) if part.dtype == jnp.float32 else in_vmem(part) for part in parts], cycle)
    return out.reshape(-1, columns)


def one_hot_places(virt):
    start = jnp.zeros(virt.shape, jnp.int32)
    for label in range(8):
        below = jnp.sum((virt < label).astype(jnp.int32), axis=1, keepdims=True)
        start = jnp.where(virt == label, below, start)
    place = lax.broadcasted_iota(jnp.int32, virt.shape, 1) - start
    return lax.broadcasted_iota(jnp.int32, (SEGMENT, BW), 0) == place


def spread_matrix(virt):
    hot = one_hot_places(virt).astype(jnp.float32)
    none = jnp.zeros_like(hot)
    group = LANES // SEGMENT
    rows = [jnp.concatenate([hot if a == b else none for b in range(group)], axis=1) for a in range(group)]
    return jnp.concatenate(rows, axis=0).astype(jnp.bfloat16)


def row_labels(occ, virt, first, rows):
    row = lax.broadcasted_iota(jnp.int32, (rows, 1), 0)
    k = first + row // PAN
    lane = lax.broadcasted_iota(jnp.int32, (rows, occ.shape[1]), 1)
    k_label = jnp.sum(jnp.where(lane == k, occ, 0), axis=1, keepdims=True)
    lane = lax.broadcasted_iota(jnp.int32, (rows, LANES), 1)
    c_label = jnp.sum(jnp.where(lane == row % PAN, virt[:, :LANES], 0), axis=1, keepdims=True)
    return k_label ^ c_label


def pack_kernel(occ_s_ref, occ_ref, virt_ref, cycle_ref, packed_ref, jb_ref):
    rows, columns = cycle_ref.shape
    virt = virt_ref[...]
    mine = row_labels(occ_ref[...], virt, lax.axis_index(OCC) * (rows // PAN), rows)
    spread = spread_matrix(virt)
    width = spread.shape[1]
    for step in range(columns // width):
        lanes = slice(step * width, (step + 1) * width)
        first = (lax.axis_index(VIR) * (columns // width) + step) * (width // BW)
        jb = jnp.concatenate([virt ^ occ_s_ref[first + jj] for jj in range(width // BW)], axis=1)
        jb_ref[:, lanes] = jb
        masked = jnp.where(mine == jb, cycle_ref[:, lanes].astype(jnp.float32), 0.0).astype(jnp.bfloat16)
        packed_ref[:, step * LANES : (step + 1) * LANES] = lax.dot_general(
            masked, spread, (((1,), (1,)), ((), ())), preferred_element_type=jnp.float32
        ).astype(jnp.bfloat16)


def pack(occ_irrep, virt_irrep, cycle_int):
    rows, columns = cycle_int.shape
    width = columns * SEGMENT // BW
    return pl.pallas_call(
        pack_kernel,
        in_specs=[SCALARS, WHOLE, WHOLE, WHOLE],
        out_shape=[
            jax.ShapeDtypeStruct((rows, width), jnp.bfloat16),
            jax.ShapeDtypeStruct((1, columns), jnp.int32),
        ],
        compiler_params=params(12),
        cost_estimate=cost(rows, LANES, columns),
        name="pack",
    )(occ_irrep, occ_irrep[None, :], virt_irrep[None, :], in_hbm(cycle_int))


def lane_labels(occ_s, virt_s, depth):
    lane = lax.broadcasted_iota(jnp.int32, (1, LANES), 1)
    c_label = jnp.zeros((1, LANES), jnp.int32)
    for c in range(PAN):
        c_label = jnp.where(lane % PAN == c, virt_s[c], c_label)
    pieces = []
    per_row = LANES // PAN
    for row in range(depth // LANES):
        k_label = jnp.zeros((1, LANES), jnp.int32)
        for m in range(per_row):
            k_label = jnp.where(lane // PAN == m, occ_s[row * per_row + m], k_label)
        pieces.append(k_label ^ c_label)
    return jnp.concatenate(pieces, axis=1)


def cycle_kernel(occ_s_ref, virt_s_ref, virt_ref, jb_ref, amp_ref, packed_ref, _, out_ref, split_ref):
    rows, depth = amp_ref.shape
    width = LANES // SEGMENT * BW

    @pl.when(pl.program_id(0) == 0)
    def _split():
        label = lane_labels(occ_s_ref, virt_s_ref, depth)
        amp = amp_ref[...].astype(jnp.float32)
        for g in range(8):
            split_ref[g * rows : (g + 1) * rows, :] = jnp.where(label == g, amp, 0.0).astype(jnp.bfloat16)

    parts = jnp.dot(split_ref[...], packed_ref[...], preferred_element_type=jnp.float32)
    spread = spread_matrix(virt_ref[...]).astype(jnp.float32)
    for pair in range(packed_ref.shape[1] // LANES):
        lanes = slice(pair * LANES, (pair + 1) * LANES)
        wide = jnp.concatenate([parts[g * rows : (g + 1) * rows, lanes] for g in range(8)], axis=1)
        high = wide.astype(jnp.bfloat16)
        low = (wide - high.astype(jnp.float32)).astype(jnp.bfloat16)
        jb = jb_ref[:, pair * width : (pair + 1) * width]
        choose = jnp.concatenate([jnp.where(jb == g, spread, 0.0).astype(jnp.bfloat16) for g in range(8)], axis=0)
        both = jnp.dot(jnp.concatenate([high, low], axis=0), choose, preferred_element_type=jnp.float32)
        out_ref[..., pair * width : (pair + 1) * width] = (both[:rows, :] + both[rows:, :]).reshape(out_ref.shape[:3] + (width,))


def cycle_term(occ_irrep, virt_irrep, jb_irrep, amp, packed, after):
    rows, depth = amp.shape
    steps = 2
    columns = jb_irrep.shape[1]
    shape = (rows // AW, AW // 8, 8, columns)
    return pl.pallas_call(
        cycle_kernel,
        grid=(steps,),
        in_specs=[
            SCALARS,
            SCALARS,
            WHOLE,
            pl.BlockSpec((1, columns // steps), lambda t: (0, t)),
            pl.BlockSpec((rows, depth), lambda t: (0, 0)),
            pl.BlockSpec((depth, packed.shape[1] // steps), lambda t: (0, t)),
            ANYWHERE,
        ],
        out_specs=pl.BlockSpec(shape[:3] + (columns // steps,), lambda t: (0, 0, 0, t)),
        out_shape=pltpu.HBM(shape, jnp.float32),
        scratch_shapes=[pltpu.VMEM((8 * rows, depth), jnp.bfloat16)],
        compiler_params=params(28),
        cost_estimate=cost(2 * rows, depth, columns),
        name="cycle_term",
    )(in_hbm(occ_irrep), in_hbm(virt_irrep), virt_irrep[None, :], jb_irrep, in_hbm(amp), in_hbm(packed), after)


def swap(value, axis):
    return lax.ppermute(value, axis, [(0, 1), (1, 0)])


def exchange(value):
    return lax.all_to_all(value, "x", 0, 0)


def dense_cycle(amp, cycle_int, occ_irrep, virt_irrep, j_first, j_width):
    gathered = lax.all_gather(cycle_int, OCC, axis=0, tiled=True)
    kc_irrep = (occ_irrep[:, None] ^ virt_irrep[None, :PAN]).reshape(-1)
    jb_irrep = lax.dynamic_slice_in_dim(occ_irrep, j_first, j_width, 0)[:, None] ^ virt_irrep[None, :]
    allowed = kc_irrep[:, None] == jb_irrep.reshape(1, -1)
    masked = jnp.where(allowed, gathered, jnp.zeros((), gathered.dtype))
    cycle = jnp.dot(amp, masked, preferred_element_type=jnp.float32)
    return cycle.reshape(amp.shape[0] // AW, AW // 8, 8, -1)


def per_device(lam, ladder_int, cycle_amp, cycle_int, occ_irrep, virt_irrep):
    j_width = JW // lax.axis_size(VIR)
    j_first = lax.axis_index(VIR) * j_width
    fits = jnp.all(virt_irrep[SEGMENT:] != virt_irrep[:-SEGMENT])
    last, jb_irrep = pack(occ_irrep, virt_irrep, cycle_int)
    gathered = lax.all_gather(last, OCC, axis=0, tiled=True)

    kinds = [kind for kind, _, _ in CHUNKS]
    widths = [a * BW for _, a, _ in CHUNKS]
    tiles = [a * BW for _, _, a in CHUNKS]
    firsts = [sum(widths[:n]) for n in range(len(CHUNKS))]
    lam_rows = {}
    core_got, sent, kept, second = {}, {}, {}, {}

    def partner(n, last):
        if not lam_rows:
            last, lam_rows["own"], lam_rows["other"] = first_partner_part(
                lam, ladder_int, firsts[n], widths[n], tiles[n], last
            )
        else:
            last = partner_part(lam_rows["other"], ladder_int, firsts[n], widths[n], tiles[n], last)
        core_got[n] = swap(last, "core")
        return last

    def own(n, last):
        args = (lam_rows["own"], ladder_int, core_got[n], firsts[n], widths[n], tiles[n], last)
        if kinds[n] == "z":
            last, kept[n] = own_z_part(*args)
            sent[n] = swap(last, "z_hi")
        else:
            last = own_x_part(*args)
            sent[n] = exchange(last)
        return last

    def merge(n, last):
        if kinds[n] == "z":
            last = merge_z(kept[n], sent[n], last)
            second[n] = [exchange(last)]
        else:
            send, last = merge_x(sent[n], tiles[n] // LANES, last)
            second[n] = [last, swap(send, "z_hi")]
        return last

    for step in ORDER:
        if step == "C":
            cycle = lax.cond(
                fits,
                lambda gathered, jb, amp, own, occ, virt, last: cycle_term(occ, virt, jb, amp, gathered, last),
                lambda gathered, jb, amp, own, occ, virt, last: dense_cycle(amp, own, occ, virt, j_first, j_width),
                *(gathered, jb_irrep, cycle_amp, cycle_int, occ_irrep, virt_irrep, last),
            )
            last = cycle
        else:
            last = {"P": partner, "O": own, "M": merge}[step[0]](int(step[1]), last)
    return finish([part for n in range(len(CHUNKS)) for part in second[n]], cycle)


def solution(mesh):
    fine = Mesh(mesh.devices.reshape(2, 4, 4, 2, 2), ("z_lo", "y", "x", "z_hi", "core"))
    return jax.shard_map(
        per_device,
        mesh=fine,
        in_specs=(P(OCC, VIR), P(VIR, None), P(OCC, None), P(OCC, VIR), P(), P()),
        out_specs=P(OCC, VIR),
        check_vma=False,
    )
```

```python
import functools

import jax
import jax.numpy as jnp
from jax import lax
from jax.experimental import pallas as pl
from jax.experimental.pallas import tpu as pltpu
from jax.sharding import Mesh, PartitionSpec as P

PAN = 16
AW = 16
BW = 256
JW = 128
LANES = 128
HALVES = BW // LANES
SCALE_ROWS = 16
SEGMENT = 64
MIB = 1024 * 1024

VIR = ("x", "z_hi", "core")
OCC = ("z_lo", "y")
CHUNKS = (("x", 10, 5), ("z", 6, 2))
ORDER = ("P0", "P1", "O0", "O1", "C", "M0", "M1")
SCALE = 8


def encode(block):
    top = jnp.maximum(jnp.max(jnp.abs(block), axis=0, keepdims=True), 1e-30)
    level = jnp.ceil(jnp.log2(top) * 256.0) + 1.0
    step = jnp.exp2(level * (-1.0 / 256.0)) * 32767.0
    return jnp.round(block * step).astype(jnp.int32).astype(jnp.int16), level


def lane_block(value, block):
    return value[:, block * LANES : (block + 1) * LANES]


def decode(code, step):
    return code.astype(jnp.int32).astype(jnp.float32) * step


def level_rows(level):
    blocks = level.shape[1] // LANES
    rows = [lane_block(level, block) for block in range(blocks)]
    spare = jnp.zeros((1, LANES), jnp.float32)
    rows = jnp.concatenate(rows + [spare] * (SCALE_ROWS - blocks), axis=0)
    return rows.astype(jnp.int32).astype(jnp.int16)


def read_steps(block):
    level = block.astype(jnp.int32).astype(jnp.float32)
    return jnp.exp2(level * (1.0 / 256.0)) * (1.0 / 32767.0)


def params(mib):
    return pltpu.CompilerParams(vmem_limit_bytes=mib * MIB)


def in_hbm(value):
    return pltpu.with_memory_space_constraint(value, pltpu.HBM)


def in_vmem(value):
    return pltpu.with_memory_space_constraint(value, pltpu.VMEM)


def cost(rows, depth, columns, more=0):
    flops, moved = 2 * rows * depth * columns, 2 * (rows * depth + depth * columns) + more
    return pl.CostEstimate(flops=flops // SCALE, bytes_accessed=moved // SCALE + 1, transcendentals=0)


ANYWHERE = pl.BlockSpec(memory_space=pl.ANY)
SCALARS = pl.BlockSpec(memory_space=pltpu.SMEM)
WHOLE = pl.BlockSpec(memory_space=pltpu.VMEM)


def product(lam_rows, panel_ref):
    return jnp.dot(lam_rows, panel_ref[...], preferred_element_type=jnp.float32)


def partner_body(lam_rows, panel_ref, out_ref):
    rows = lam_rows.shape[0]
    acc = product(lam_rows, panel_ref)
    blocks = acc.shape[1] // LANES
    code, level = encode(acc)
    for block in range(blocks):
        out_ref[0, block * rows : (block + 1) * rows, :] = lane_block(code, block)
    out_ref[0, blocks * rows :, :] = level_rows(level)


def first_partner_kernel(lam_ref, panel_ref, _, out_ref, own_ref, other_ref):
    @pl.when(pl.program_id(0) == 0)
    def _select():
        here = lax.axis_index("core")
        for part in range(lam_ref.shape[0] // 32):
            rows = lam_ref[part * 32 : (part + 1) * 32, :].astype(jnp.float32)
            low = jnp.concatenate([rows[0:8], rows[16:24]], axis=0)
            high = jnp.concatenate([rows[8:16], rows[24:32]], axis=0)
            at = slice(part * 16, (part + 1) * 16)
            own_ref[at, :] = jnp.where(here == 0, low, high).astype(jnp.bfloat16)
            other_ref[at, :] = jnp.where(here == 0, high, low).astype(jnp.bfloat16)

    partner_body(other_ref[...], panel_ref, out_ref)


def first_partner_part(lam, panel, first, width, tile, after):
    rows, depth = lam.shape
    half = rows // 2
    tiles, offset = width // tile, first // tile
    size = tile // LANES * half + SCALE_ROWS
    return pl.pallas_call(
        first_partner_kernel,
        grid=(tiles,),
        in_specs=[
            pl.BlockSpec((rows, depth), lambda t: (0, 0)),
            pl.BlockSpec((depth, tile), lambda t: (0, t + offset)),
            ANYWHERE,
        ],
        out_specs=[
            pl.BlockSpec((1, size, LANES), lambda t: (t, 0, 0)),
            WHOLE,
            WHOLE,
        ],
        out_shape=[
            jax.ShapeDtypeStruct((tiles, size, LANES), jnp.int16),
            pltpu.VMEM((half, depth), jnp.bfloat16),
            pltpu.VMEM((half, depth), jnp.bfloat16),
        ],
        compiler_params=params(36),
        cost_estimate=cost(half, depth, width),
        name="partner_part",
    )(in_hbm(lam), in_hbm(panel), after)


def partner_kernel(lam_ref, panel_ref, _, out_ref):
    partner_body(lam_ref[...], panel_ref, out_ref)


def partner_part(lam_rows, panel, first, width, tile, after):
    rows, depth = lam_rows.shape
    tiles, offset = width // tile, first // tile
    size = tile // LANES * rows + SCALE_ROWS
    return pl.pallas_call(
        partner_kernel,
        grid=(tiles,),
        in_specs=[
            WHOLE,
            pl.BlockSpec((depth, tile), lambda t: (0, t + offset)),
            ANYWHERE,
        ],
        out_specs=pl.BlockSpec((1, size, LANES), lambda t: (t, 0, 0)),
        out_shape=jax.ShapeDtypeStruct((tiles, size, LANES), jnp.int16),
        compiler_params=params(20),
        cost_estimate=cost(rows, depth, width),
        name="partner_part",
    )(in_vmem(lam_rows), in_vmem(panel), after)


def own_sum(lam_ref, panel_ref, recv_ref):
    rows = lam_ref.shape[0]
    acc = product(lam_ref[...], panel_ref)
    blocks = acc.shape[1] // LANES
    tile = pl.program_id(0)
    steps = read_steps(recv_ref[tile, blocks * rows :, :])
    got = [
        decode(recv_ref[tile, block * rows : (block + 1) * rows, :], steps[block : block + 1, :])
        for block in range(blocks)
    ]
    return acc + jnp.concatenate(got, axis=1)


def target_rows(total, x_dev, z_dev, i_dev):
    pieces = [total[(i * 8 + x_dev * 2 + z_dev) * 8 : (i * 8 + x_dev * 2 + z_dev) * 8 + 8, :] for i in range(i_dev)]
    return jnp.concatenate(pieces, axis=0)


def own_z_kernel(lam_ref, panel_ref, recv_ref, _, send_ref, keep_ref):
    i_dev = lam_ref.shape[0] // 64
    here = lax.axis_index("z_hi")
    total = own_sum(lam_ref, panel_ref, recv_ref)
    blocks = total.shape[1] // LANES
    size = 4 * i_dev * 8
    low = jnp.concatenate([target_rows(total, x, 0, i_dev) for x in range(4)], axis=0)
    high = jnp.concatenate([target_rows(total, x, 1, i_dev) for x in range(4)], axis=0)
    keep = jnp.where(here == 0, low, high)
    code, level = encode(jnp.where(here == 0, high, low))
    for block in range(blocks):
        keep_ref[0, block] = lane_block(keep, block)
        send_ref[0, block * size : (block + 1) * size, :] = lane_block(code, block)
    send_ref[0, blocks * size :, :] = level_rows(level)


def own_z_part(lam_rows, panel, recv, first, width, tile, after):
    rows, depth = lam_rows.shape
    tiles, offset = width // tile, first // tile
    blocks = tile // LANES
    size = blocks * (rows // 2) + SCALE_ROWS
    return pl.pallas_call(
        own_z_kernel,
        grid=(tiles,),
        in_specs=[
            pl.BlockSpec((rows, depth), lambda t: (0, 0)),
            pl.BlockSpec((depth, tile), lambda t: (0, t + offset)),
            WHOLE,
            ANYWHERE,
        ],
        out_specs=[
            pl.BlockSpec((1, size, LANES), lambda t: (t, 0, 0)),
            pl.BlockSpec((1, blocks, rows // 2, LANES), lambda t: (t, 0, 0, 0)),
        ],
        out_shape=[
            jax.ShapeDtypeStruct((tiles, size, LANES), jnp.int16),
            pltpu.HBM((tiles, blocks, rows // 2, LANES), jnp.float32),
        ],
        compiler_params=params(26),
        cost_estimate=cost(rows, depth, width),
        name="own_z_part",
    )(in_hbm(lam_rows), in_hbm(panel), recv, after)


def own_x_kernel(lam_ref, panel_ref, recv_ref, _, send_ref):
    i_dev = lam_ref.shape[0] // 64
    total = own_sum(lam_ref, panel_ref, recv_ref)
    blocks = total.shape[1] // LANES
    size = 2 * i_dev * 8
    for x in range(4):
        code, level = encode(jnp.concatenate([target_rows(total, x, z, i_dev) for z in range(2)], axis=0))
        for block in range(blocks):
            send_ref[x, 0, block * size : (block + 1) * size, :] = lane_block(code, block)
        send_ref[x, 0, blocks * size :, :] = level_rows(level)


def own_x_part(lam_rows, panel, recv, first, width, tile, after):
    rows, depth = lam_rows.shape
    tiles, offset = width // tile, first // tile
    blocks = tile // LANES
    size = blocks * (rows // 4) + SCALE_ROWS
    return pl.pallas_call(
        own_x_kernel,
        grid=(tiles,),
        in_specs=[
            WHOLE,
            pl.BlockSpec((depth, tile), lambda t: (0, t + offset)),
            WHOLE,
            ANYWHERE,
        ],
        out_specs=pl.BlockSpec((4, 1, size, LANES), lambda t: (0, t, 0, 0)),
        out_shape=jax.ShapeDtypeStruct((4, tiles, size, LANES), jnp.int16),
        compiler_params=params(26),
        cost_estimate=cost(rows, depth, width),
        name="own_x_part",
    )(in_vmem(lam_rows), in_vmem(panel), recv, after)


def merge_z_kernel(keep_ref, recv_ref, _, send_ref):
    blocks, rows = keep_ref.shape[1:3]
    owner = rows // 4
    tile = pl.program_id(0)
    steps = read_steps(recv_ref[tile, blocks * rows :, :])
    totals = []
    for x in range(4):
        for block in range(blocks):
            part = slice(block * rows + x * owner, block * rows + (x + 1) * owner)
            got = decode(recv_ref[tile, part, :], steps[block : block + 1, :])
            totals.append(keep_ref[tile, block, x * owner : (x + 1) * owner, :] + got)
    code, level = encode(jnp.concatenate(totals, axis=1))
    for x in range(4):
        for block in range(blocks):
            send_ref[x, 0, block * owner : (block + 1) * owner, :] = lane_block(code, x * blocks + block)
        mine = slice(x * blocks * LANES, (x + 1) * blocks * LANES)
        send_ref[x, 0, blocks * owner :, :] = level_rows(level[:, mine])


def merge_z(keep, recv, after):
    tiles, blocks, rows, _ = keep.shape
    size = blocks * (rows // 4) + SCALE_ROWS
    return pl.pallas_call(
        merge_z_kernel,
        grid=(tiles,),
        in_specs=[
            WHOLE,
            WHOLE,
            ANYWHERE,
        ],
        out_specs=pl.BlockSpec((4, 1, size, LANES), lambda t: (0, t, 0, 0)),
        out_shape=jax.ShapeDtypeStruct((4, tiles, size, LANES), jnp.int16),
        compiler_params=params(10),
        cost_estimate=cost(0, 0, 0, 6 * keep.size + 2 * recv.size),
        name="merge_z",
    )(in_vmem(keep), recv, in_hbm(after))


def merge_x_kernel(recv_ref, _, send_ref, keep_ref):
    sources = recv_ref.shape[0]
    tile = pl.program_id(0)
    blocks, owner = keep_ref.shape[1:3]
    rows = 2 * owner
    here = lax.axis_index("z_hi")
    steps = [read_steps(recv_ref[s, tile, blocks * rows :, :]) for s in range(sources)]
    sends = []
    for block in range(blocks):
        part = slice(block * rows, (block + 1) * rows)
        total = sum(decode(recv_ref[s, tile, part, :], steps[s][block : block + 1, :]) for s in range(sources))
        low, high = total[:owner, :], total[owner:, :]
        keep_ref[0, block] = jnp.where(here == 0, low, high)
        sends.append(jnp.where(here == 0, high, low))
    code, level = encode(jnp.concatenate(sends, axis=1))
    for block in range(blocks):
        send_ref[0, block * owner : (block + 1) * owner, :] = lane_block(code, block)
    send_ref[0, blocks * owner :, :] = level_rows(level)


def merge_x(recv, blocks, after):
    sources, tiles, size, _ = recv.shape
    owner = (size - SCALE_ROWS) // blocks // 2
    return pl.pallas_call(
        merge_x_kernel,
        grid=(tiles,),
        in_specs=[
            WHOLE,
            ANYWHERE,
        ],
        out_specs=[
            pl.BlockSpec((1, blocks * owner + SCALE_ROWS, LANES), lambda t: (t, 0, 0)),
            pl.BlockSpec((1, blocks, owner, LANES), lambda t: (t, 0, 0, 0)),
        ],
        out_shape=[
            pltpu.HBM((tiles, blocks * owner + SCALE_ROWS, LANES), jnp.int16),
            pltpu.HBM((tiles, blocks, owner, LANES), jnp.float32),
        ],
        compiler_params=params(10),
        cost_estimate=cost(0, 0, 0, 2 * recv.size),
        name="merge_x",
    )(recv, after)


def finish_kernel(*refs):
    cycle_ref, out_ref = refs[-2:]
    refs = refs[:-2]
    rows = JW // 16 * 8
    i_dev = rows // 8
    blocks = []
    for kind, _, tile_a in CHUNKS:
        count = tile_a * HALVES
        if kind == "z":
            recv_ref, refs = refs[0], refs[1:]
            sources, tiles = recv_ref.shape[:2]
            for tile in range(tiles):
                levels = [read_steps(recv_ref[s, tile, count * rows :, :]) for s in range(sources)]

                def summed(block, ref=recv_ref, tile=tile, levels=levels):
                    part = slice(block * rows, (block + 1) * rows)
                    return sum(
                        decode(ref[s, tile, part, :], levels[s][block : block + 1, :]) for s in range(len(levels))
                    )

                blocks += [functools.partial(summed, block) for block in range(count)]
        else:
            (keep_ref, recv_ref), refs = refs[:2], refs[2:]
            for tile in range(recv_ref.shape[0]):
                levels = read_steps(recv_ref[tile, count * rows :, :])

                def kept(block, keep=keep_ref, ref=recv_ref, tile=tile, levels=levels):
                    part = slice(block * rows, (block + 1) * rows)
                    return keep[tile, block] + decode(ref[tile, part, :], levels[block : block + 1, :])

                blocks += [functools.partial(kept, block) for block in range(count)]

    for group in range(AW // 8):

        @pl.when(pl.program_id(0) == group)
        def _group(group=group):
            for half in range(HALVES):
                totals = [blocks[(group * 8 + a) * HALVES + half]() for a in range(8)]
                for i in range(i_dev):
                    stack = jnp.stack([total[i * 8 : (i + 1) * 8, :] for total in totals], axis=0)
                    turned = jnp.swapaxes(stack, 0, 1)
                    for jj in range(8):
                        lanes = pl.ds(jj * BW + half * LANES, LANES)
                        out_ref[i, 0, :, lanes] = turned[jj] + cycle_ref[i, 0, :, lanes]


def finish(parts, cycle):
    shape = cycle.shape
    columns = shape[-1]
    block = pl.BlockSpec((shape[0], 1, 8, columns), lambda t: (0, t, 0, 0))
    out = pl.pallas_call(
        finish_kernel,
        grid=(AW // 8,),
        in_specs=[WHOLE] * len(parts) + [block],
        out_specs=block,
        out_shape=pltpu.HBM(shape, jnp.float32),
        compiler_params=params(12),
        cost_estimate=cost(0, 0, 0, 16 * cycle.size),
        name="finish",
    )(*[in_hbm(part) if part.dtype == jnp.float32 else in_vmem(part) for part in parts], cycle)
    return out.reshape(-1, columns)


def one_hot_places(virt):
    start = jnp.zeros(virt.shape, jnp.int32)
    for label in range(8):
        below = jnp.sum((virt < label).astype(jnp.int32), axis=1, keepdims=True)
        start = jnp.where(virt == label, below, start)
    place = lax.broadcasted_iota(jnp.int32, virt.shape, 1) - start
    return lax.broadcasted_iota(jnp.int32, (SEGMENT, BW), 0) == place


def spread_matrix(virt):
    hot = one_hot_places(virt).astype(jnp.float32)
    none = jnp.zeros_like(hot)
    group = LANES // SEGMENT
    rows = [jnp.concatenate([hot if a == b else none for b in range(group)], axis=1) for a in range(group)]
    return jnp.concatenate(rows, axis=0).astype(jnp.bfloat16)


def row_labels(occ, virt, first, rows):
    row = lax.broadcasted_iota(jnp.int32, (rows, 1), 0)
    k = first + row // PAN
    lane = lax.broadcasted_iota(jnp.int32, (rows, occ.shape[1]), 1)
    k_label = jnp.sum(jnp.where(lane == k, occ, 0), axis=1, keepdims=True)
    lane = lax.broadcasted_iota(jnp.int32, (rows, LANES), 1)
    c_label = jnp.sum(jnp.where(lane == row % PAN, virt[:, :LANES], 0), axis=1, keepdims=True)
    return k_label ^ c_label


def pack_kernel(occ_s_ref, occ_ref, virt_ref, cycle_ref, packed_ref, jb_ref, held_ref, sems):
    rows, columns = held_ref.shape
    width = LANES // SEGMENT * BW
    steps = columns // width
    copies = [
        pltpu.make_async_copy(
            cycle_ref.at[:, pl.ds(step * width, width)], held_ref.at[:, pl.ds(step * width, width)], sems.at[step]
        )
        for step in range(steps)
    ]
    for copy in copies:
        copy.start()
    virt = virt_ref[...]
    mine = row_labels(occ_ref[...], virt, lax.axis_index(OCC) * (rows // PAN), rows)
    spread = spread_matrix(virt)
    for step in range(steps):
        lanes = slice(step * width, (step + 1) * width)
        first = (lax.axis_index(VIR) * steps + step) * (width // BW)
        jb = jnp.concatenate([virt ^ occ_s_ref[first + jj] for jj in range(width // BW)], axis=1)
        jb_ref[:, lanes] = jb
        copies[step].wait()
        masked = jnp.where(mine == jb, held_ref[:, lanes].astype(jnp.float32), 0.0).astype(jnp.bfloat16)
        packed_ref[:, step * LANES : (step + 1) * LANES] = lax.dot_general(
            masked, spread, (((1,), (1,)), ((), ())), preferred_element_type=jnp.float32
        ).astype(jnp.bfloat16)


def pack(occ_irrep, virt_irrep, cycle_int):
    rows, columns = cycle_int.shape
    width = columns * SEGMENT // BW
    return pl.pallas_call(
        pack_kernel,
        in_specs=[SCALARS, WHOLE, WHOLE, ANYWHERE],
        out_shape=[
            jax.ShapeDtypeStruct((rows, width), jnp.bfloat16),
            jax.ShapeDtypeStruct((1, columns), jnp.int32),
        ],
        scratch_shapes=[
            pltpu.VMEM((rows, columns), jnp.bfloat16),
            pltpu.SemaphoreType.DMA((columns * SEGMENT // BW // LANES,)),
        ],
        compiler_params=params(12),
        cost_estimate=cost(rows, LANES, columns),
        name="pack",
    )(occ_irrep, occ_irrep[None, :], virt_irrep[None, :], in_hbm(cycle_int))


def lane_labels(occ_s, virt_s, depth):
    lane = lax.broadcasted_iota(jnp.int32, (1, LANES), 1)
    c_label = jnp.zeros((1, LANES), jnp.int32)
    for c in range(PAN):
        c_label = jnp.where(lane % PAN == c, virt_s[c], c_label)
    pieces = []
    per_row = LANES // PAN
    for row in range(depth // LANES):
        k_label = jnp.zeros((1, LANES), jnp.int32)
        for m in range(per_row):
            k_label = jnp.where(lane // PAN == m, occ_s[row * per_row + m], k_label)
        pieces.append(k_label ^ c_label)
    return jnp.concatenate(pieces, axis=1)


def cycle_kernel(occ_s_ref, virt_s_ref, virt_ref, jb_ref, amp_ref, packed_ref, _, out_ref, split_ref):
    rows, depth = amp_ref.shape
    width = LANES // SEGMENT * BW

    @pl.when(pl.program_id(0) == 0)
    def _split():
        label = lane_labels(occ_s_ref, virt_s_ref, depth)
        amp = amp_ref[...].astype(jnp.float32)
        for g in range(8):
            split_ref[g * rows : (g + 1) * rows, :] = jnp.where(label == g, amp, 0.0).astype(jnp.bfloat16)

    parts = jnp.dot(split_ref[...], packed_ref[...], preferred_element_type=jnp.float32)
    spread = spread_matrix(virt_ref[...]).astype(jnp.float32)
    for pair in range(packed_ref.shape[1] // LANES):
        lanes = slice(pair * LANES, (pair + 1) * LANES)
        wide = jnp.concatenate([parts[g * rows : (g + 1) * rows, lanes] for g in range(8)], axis=1)
        high = wide.astype(jnp.bfloat16)
        low = (wide - high.astype(jnp.float32)).astype(jnp.bfloat16)
        jb = jb_ref[:, pair * width : (pair + 1) * width]
        choose = jnp.concatenate([jnp.where(jb == g, spread, 0.0).astype(jnp.bfloat16) for g in range(8)], axis=0)
        both = jnp.dot(jnp.concatenate([high, low], axis=0), choose, preferred_element_type=jnp.float32)
        out_ref[..., pair * width : (pair + 1) * width] = (both[:rows, :] + both[rows:, :]).reshape(out_ref.shape[:3] + (width,))


def cycle_term(occ_irrep, virt_irrep, jb_irrep, amp, packed, after):
    rows, depth = amp.shape
    steps = 2
    columns = jb_irrep.shape[1]
    shape = (rows // AW, AW // 8, 8, columns)
    return pl.pallas_call(
        cycle_kernel,
        grid=(steps,),
        in_specs=[
            SCALARS,
            SCALARS,
            WHOLE,
            pl.BlockSpec((1, columns // steps), lambda t: (0, t)),
            pl.BlockSpec((rows, depth), lambda t: (0, 0)),
            pl.BlockSpec((depth, packed.shape[1] // steps), lambda t: (0, t)),
            ANYWHERE,
        ],
        out_specs=pl.BlockSpec(shape[:3] + (columns // steps,), lambda t: (0, 0, 0, t)),
        out_shape=pltpu.HBM(shape, jnp.float32),
        scratch_shapes=[pltpu.VMEM((8 * rows, depth), jnp.bfloat16)],
        compiler_params=params(28),
        cost_estimate=cost(2 * rows, depth, columns),
        name="cycle_term",
    )(in_hbm(occ_irrep), in_hbm(virt_irrep), virt_irrep[None, :], jb_irrep, in_hbm(amp), in_hbm(packed), after)


def swap(value, axis):
    return lax.ppermute(value, axis, [(0, 1), (1, 0)])


def exchange(value):
    return lax.all_to_all(value, "x", 0, 0)


def dense_cycle(amp, cycle_int, occ_irrep, virt_irrep, j_first, j_width):
    gathered = lax.all_gather(cycle_int, OCC, axis=0, tiled=True)
    kc_irrep = (occ_irrep[:, None] ^ virt_irrep[None, :PAN]).reshape(-1)
    jb_irrep = lax.dynamic_slice_in_dim(occ_irrep, j_first, j_width, 0)[:, None] ^ virt_irrep[None, :]
    allowed = kc_irrep[:, None] == jb_irrep.reshape(1, -1)
    masked = jnp.where(allowed, gathered, jnp.zeros((), gathered.dtype))
    cycle = jnp.dot(amp, masked, preferred_element_type=jnp.float32)
    return cycle.reshape(amp.shape[0] // AW, AW // 8, 8, -1)


def per_device(lam, ladder_int, cycle_amp, cycle_int, occ_irrep, virt_irrep):
    j_width = JW // lax.axis_size(VIR)
    j_first = lax.axis_index(VIR) * j_width
    fits = jnp.all(virt_irrep[SEGMENT:] != virt_irrep[:-SEGMENT])
    last, jb_irrep = pack(occ_irrep, virt_irrep, cycle_int)
    gathered = lax.all_gather(last, OCC, axis=0, tiled=True)

    kinds = [kind for kind, _, _ in CHUNKS]
    widths = [a * BW for _, a, _ in CHUNKS]
    tiles = [a * BW for _, _, a in CHUNKS]
    firsts = [sum(widths[:n]) for n in range(len(CHUNKS))]
    lam_rows = {}
    core_got, sent, kept, second = {}, {}, {}, {}

    def partner(n, last):
        if not lam_rows:
            last, lam_rows["own"], lam_rows["other"] = first_partner_part(
                lam, ladder_int, firsts[n], widths[n], tiles[n], last
            )
        else:
            last = partner_part(lam_rows["other"], ladder_int, firsts[n], widths[n], tiles[n], last)
        core_got[n] = swap(last, "core")
        return last

    def own(n, last):
        args = (lam_rows["own"], ladder_int, core_got[n], firsts[n], widths[n], tiles[n], last)
        if kinds[n] == "z":
            last, kept[n] = own_z_part(*args)
            sent[n] = swap(last, "z_hi")
        else:
            last = own_x_part(*args)
            sent[n] = exchange(last)
        return last

    def merge(n, last):
        if kinds[n] == "z":
            last = merge_z(kept[n], sent[n], last)
            second[n] = [exchange(last)]
        else:
            send, last = merge_x(sent[n], tiles[n] // LANES, last)
            second[n] = [last, swap(send, "z_hi")]
        return last

    for step in ORDER:
        if step == "C":
            cycle = lax.cond(
                fits,
                lambda gathered, jb, amp, own, occ, virt, last: cycle_term(occ, virt, jb, amp, gathered, last),
                lambda gathered, jb, amp, own, occ, virt, last: dense_cycle(amp, own, occ, virt, j_first, j_width),
                *(gathered, jb_irrep, cycle_amp, cycle_int, occ_irrep, virt_irrep, last),
            )
            last = cycle
        else:
            last = {"P": partner, "O": own, "M": merge}[step[0]](int(step[1]), last)
    return finish([part for n in range(len(CHUNKS)) for part in second[n]], cycle)


def solution(mesh):
    fine = Mesh(mesh.devices.reshape(2, 4, 4, 2, 2), ("z_lo", "y", "x", "z_hi", "core"))
    return jax.shard_map(
        per_device,
        mesh=fine,
        in_specs=(P(OCC, VIR), P(VIR, None), P(OCC, None), P(OCC, VIR), P(), P()),
        out_specs=P(OCC, VIR),
        check_vma=False,
    )
```

```python
import functools

import jax
import jax.numpy as jnp
from jax import lax
from jax.experimental import pallas as pl
from jax.experimental.pallas import tpu as pltpu
from jax.sharding import Mesh, PartitionSpec as P

PAN = 16
AW = 16
BW = 256
JW = 128
LANES = 128
HALVES = BW // LANES
SCALE_ROWS = 16
SEGMENT = 64
MIB = 1024 * 1024

VIR = ("x", "z_hi", "core")
OCC = ("z_lo", "y")
CHUNKS = (("x", 10, 5), ("z", 6, 2))
ORDER = ("P0", "P1", "O0", "O1", "C", "M0", "M1")
SCALE = 8


def encode(block):
    top = jnp.maximum(jnp.max(jnp.abs(block), axis=0, keepdims=True), 1e-30)
    level = jnp.ceil(jnp.log2(top) * 256.0) + 1.0
    step = jnp.exp2(level * (-1.0 / 256.0)) * 32767.0
    return jnp.round(block * step).astype(jnp.int32).astype(jnp.int16), level


def lane_block(value, block):
    return value[:, block * LANES : (block + 1) * LANES]


def decode(code, step):
    return code.astype(jnp.int32).astype(jnp.float32) * step


def level_rows(level):
    blocks = level.shape[1] // LANES
    rows = [lane_block(level, block) for block in range(blocks)]
    spare = jnp.zeros((1, LANES), jnp.float32)
    rows = jnp.concatenate(rows + [spare] * (SCALE_ROWS - blocks), axis=0)
    return rows.astype(jnp.int32).astype(jnp.int16)


def read_steps(block):
    level = block.astype(jnp.int32).astype(jnp.float32)
    return jnp.exp2(level * (1.0 / 256.0)) * (1.0 / 32767.0)


def params(mib):
    return pltpu.CompilerParams(vmem_limit_bytes=mib * MIB)


def in_hbm(value):
    return pltpu.with_memory_space_constraint(value, pltpu.HBM)


def in_vmem(value):
    return pltpu.with_memory_space_constraint(value, pltpu.VMEM)


def cost(rows, depth, columns, more=0):
    flops, moved = 2 * rows * depth * columns, 2 * (rows * depth + depth * columns) + more
    return pl.CostEstimate(flops=flops // SCALE, bytes_accessed=moved // SCALE + 1, transcendentals=0)


ANYWHERE = pl.BlockSpec(memory_space=pl.ANY)
SCALARS = pl.BlockSpec(memory_space=pltpu.SMEM)
WHOLE = pl.BlockSpec(memory_space=pltpu.VMEM)


def product(lam_rows, panel_ref):
    return jnp.dot(lam_rows, panel_ref[...], preferred_element_type=jnp.float32)


def partner_body(lam_rows, panel_ref, out_ref):
    rows = lam_rows.shape[0]
    acc = product(lam_rows, panel_ref)
    blocks = acc.shape[1] // LANES
    code, level = encode(acc)
    for block in range(blocks):
        out_ref[0, block * rows : (block + 1) * rows, :] = lane_block(code, block)
    out_ref[0, blocks * rows :, :] = level_rows(level)


def first_partner_kernel(lam_ref, panel_ref, _, out_ref, own_ref, other_ref):
    @pl.when(pl.program_id(0) == 0)
    def _select():
        here = lax.axis_index("core")
        for part in range(lam_ref.shape[0] // 32):
            rows = lam_ref[part * 32 : (part + 1) * 32, :].astype(jnp.float32)
            low = jnp.concatenate([rows[0:8], rows[16:24]], axis=0)
            high = jnp.concatenate([rows[8:16], rows[24:32]], axis=0)
            at = slice(part * 16, (part + 1) * 16)
            own_ref[at, :] = jnp.where(here == 0, low, high).astype(jnp.bfloat16)
            other_ref[at, :] = jnp.where(here == 0, high, low).astype(jnp.bfloat16)

    partner_body(other_ref[...], panel_ref, out_ref)


def first_partner_part(lam, panel, first, width, tile, after):
    rows, depth = lam.shape
    half = rows // 2
    tiles, offset = width // tile, first // tile
    size = tile // LANES * half + SCALE_ROWS
    return pl.pallas_call(
        first_partner_kernel,
        grid=(tiles,),
        in_specs=[
            pl.BlockSpec((rows, depth), lambda t: (0, 0)),
            pl.BlockSpec((depth, tile), lambda t: (0, t + offset)),
            ANYWHERE,
        ],
        out_specs=[
            pl.BlockSpec((1, size, LANES), lambda t: (t, 0, 0)),
            WHOLE,
            WHOLE,
        ],
        out_shape=[
            jax.ShapeDtypeStruct((tiles, size, LANES), jnp.int16),
            pltpu.VMEM((half, depth), jnp.bfloat16),
            pltpu.VMEM((half, depth), jnp.bfloat16),
        ],
        compiler_params=params(36),
        cost_estimate=cost(half, depth, width),
        name="partner_part",
    )(in_hbm(lam), in_hbm(panel), after)


def partner_kernel(lam_ref, panel_ref, _, out_ref):
    partner_body(lam_ref[...], panel_ref, out_ref)


def partner_part(lam_rows, panel, first, width, tile, after):
    rows, depth = lam_rows.shape
    tiles, offset = width // tile, first // tile
    size = tile // LANES * rows + SCALE_ROWS
    return pl.pallas_call(
        partner_kernel,
        grid=(tiles,),
        in_specs=[
            WHOLE,
            pl.BlockSpec((depth, tile), lambda t: (0, t + offset)),
            ANYWHERE,
        ],
        out_specs=pl.BlockSpec((1, size, LANES), lambda t: (t, 0, 0)),
        out_shape=jax.ShapeDtypeStruct((tiles, size, LANES), jnp.int16),
        compiler_params=params(20),
        cost_estimate=cost(rows, depth, width),
        name="partner_part",
    )(in_vmem(lam_rows), in_vmem(panel), after)


def own_sum(lam_ref, panel_ref, recv_ref):
    rows = lam_ref.shape[0]
    acc = product(lam_ref[...], panel_ref)
    blocks = acc.shape[1] // LANES
    tile = pl.program_id(0)
    steps = read_steps(recv_ref[tile, blocks * rows :, :])
    got = [
        decode(recv_ref[tile, block * rows : (block + 1) * rows, :], steps[block : block + 1, :])
        for block in range(blocks)
    ]
    return acc + jnp.concatenate(got, axis=1)


def target_rows(total, x_dev, z_dev, i_dev):
    pieces = [total[(i * 8 + x_dev * 2 + z_dev) * 8 : (i * 8 + x_dev * 2 + z_dev) * 8 + 8, :] for i in range(i_dev)]
    return jnp.concatenate(pieces, axis=0)


def own_z_kernel(lam_ref, panel_ref, recv_ref, _, send_ref, keep_ref):
    i_dev = lam_ref.shape[0] // 64
    here = lax.axis_index("z_hi")
    total = own_sum(lam_ref, panel_ref, recv_ref)
    blocks = total.shape[1] // LANES
    size = 4 * i_dev * 8
    low = jnp.concatenate([target_rows(total, x, 0, i_dev) for x in range(4)], axis=0)
    high = jnp.concatenate([target_rows(total, x, 1, i_dev) for x in range(4)], axis=0)
    keep = jnp.where(here == 0, low, high)
    code, level = encode(jnp.where(here == 0, high, low))
    for block in range(blocks):
        keep_ref[0, block] = lane_block(keep, block)
        send_ref[0, block * size : (block + 1) * size, :] = lane_block(code, block)
    send_ref[0, blocks * size :, :] = level_rows(level)


def own_z_part(lam_rows, panel, recv, first, width, tile, after):
    rows, depth = lam_rows.shape
    tiles, offset = width // tile, first // tile
    blocks = tile // LANES
    size = blocks * (rows // 2) + SCALE_ROWS
    return pl.pallas_call(
        own_z_kernel,
        grid=(tiles,),
        in_specs=[
            pl.BlockSpec((rows, depth), lambda t: (0, 0)),
            pl.BlockSpec((depth, tile), lambda t: (0, t + offset)),
            WHOLE,
            ANYWHERE,
        ],
        out_specs=[
            pl.BlockSpec((1, size, LANES), lambda t: (t, 0, 0)),
            pl.BlockSpec((1, blocks, rows // 2, LANES), lambda t: (t, 0, 0, 0)),
        ],
        out_shape=[
            jax.ShapeDtypeStruct((tiles, size, LANES), jnp.int16),
            pltpu.HBM((tiles, blocks, rows // 2, LANES), jnp.float32),
        ],
        compiler_params=params(26),
        cost_estimate=cost(rows, depth, width),
        name="own_z_part",
    )(in_hbm(lam_rows), in_hbm(panel), recv, after)


def own_x_kernel(lam_ref, panel_ref, recv_ref, _, send_ref):
    i_dev = lam_ref.shape[0] // 64
    total = own_sum(lam_ref, panel_ref, recv_ref)
    blocks = total.shape[1] // LANES
    size = 2 * i_dev * 8
    for x in range(4):
        code, level = encode(jnp.concatenate([target_rows(total, x, z, i_dev) for z in range(2)], axis=0))
        for block in range(blocks):
            send_ref[x, 0, block * size : (block + 1) * size, :] = lane_block(code, block)
        send_ref[x, 0, blocks * size :, :] = level_rows(level)


def own_x_part(lam_rows, panel, recv, first, width, tile, after):
    rows, depth = lam_rows.shape
    tiles, offset = width // tile, first // tile
    blocks = tile // LANES
    size = blocks * (rows // 4) + SCALE_ROWS
    return pl.pallas_call(
        own_x_kernel,
        grid=(tiles,),
        in_specs=[
            WHOLE,
            pl.BlockSpec((depth, tile), lambda t: (0, t + offset)),
            WHOLE,
            ANYWHERE,
        ],
        out_specs=pl.BlockSpec((4, 1, size, LANES), lambda t: (0, t, 0, 0)),
        out_shape=jax.ShapeDtypeStruct((4, tiles, size, LANES), jnp.int16),
        compiler_params=params(26),
        cost_estimate=cost(rows, depth, width),
        name="own_x_part",
    )(in_vmem(lam_rows), in_vmem(panel), recv, after)


def merge_z_kernel(keep_ref, recv_ref, _, send_ref):
    blocks, rows = keep_ref.shape[1:3]
    owner = rows // 4
    tile = pl.program_id(0)
    steps = read_steps(recv_ref[tile, blocks * rows :, :])
    totals = []
    for x in range(4):
        for block in range(blocks):
            part = slice(block * rows + x * owner, block * rows + (x + 1) * owner)
            got = decode(recv_ref[tile, part, :], steps[block : block + 1, :])
            totals.append(keep_ref[tile, block, x * owner : (x + 1) * owner, :] + got)
    code, level = encode(jnp.concatenate(totals, axis=1))
    for x in range(4):
        for block in range(blocks):
            send_ref[x, 0, block * owner : (block + 1) * owner, :] = lane_block(code, x * blocks + block)
        mine = slice(x * blocks * LANES, (x + 1) * blocks * LANES)
        send_ref[x, 0, blocks * owner :, :] = level_rows(level[:, mine])


def merge_z(keep, recv, after):
    tiles, blocks, rows, _ = keep.shape
    size = blocks * (rows // 4) + SCALE_ROWS
    return pl.pallas_call(
        merge_z_kernel,
        grid=(tiles,),
        in_specs=[
            WHOLE,
            WHOLE,
            ANYWHERE,
        ],
        out_specs=pl.BlockSpec((4, 1, size, LANES), lambda t: (0, t, 0, 0)),
        out_shape=jax.ShapeDtypeStruct((4, tiles, size, LANES), jnp.int16),
        compiler_params=params(10),
        cost_estimate=cost(0, 0, 0, 6 * keep.size + 2 * recv.size),
        name="merge_z",
    )(in_vmem(keep), recv, in_hbm(after))


def merge_x_kernel(recv_ref, _, send_ref, keep_ref):
    sources = recv_ref.shape[0]
    tile = pl.program_id(0)
    blocks, owner = keep_ref.shape[1:3]
    rows = 2 * owner
    here = lax.axis_index("z_hi")
    steps = [read_steps(recv_ref[s, tile, blocks * rows :, :]) for s in range(sources)]
    sends = []
    for block in range(blocks):
        part = slice(block * rows, (block + 1) * rows)
        total = sum(decode(recv_ref[s, tile, part, :], steps[s][block : block + 1, :]) for s in range(sources))
        low, high = total[:owner, :], total[owner:, :]
        keep_ref[0, block] = jnp.where(here == 0, low, high)
        sends.append(jnp.where(here == 0, high, low))
    code, level = encode(jnp.concatenate(sends, axis=1))
    for block in range(blocks):
        send_ref[0, block * owner : (block + 1) * owner, :] = lane_block(code, block)
    send_ref[0, blocks * owner :, :] = level_rows(level)


def merge_x(recv, blocks, after):
    sources, tiles, size, _ = recv.shape
    owner = (size - SCALE_ROWS) // blocks // 2
    return pl.pallas_call(
        merge_x_kernel,
        grid=(tiles,),
        in_specs=[
            WHOLE,
            ANYWHERE,
        ],
        out_specs=[
            pl.BlockSpec((1, blocks * owner + SCALE_ROWS, LANES), lambda t: (t, 0, 0)),
            pl.BlockSpec((1, blocks, owner, LANES), lambda t: (t, 0, 0, 0)),
        ],
        out_shape=[
            pltpu.HBM((tiles, blocks * owner + SCALE_ROWS, LANES), jnp.int16),
            pltpu.HBM((tiles, blocks, owner, LANES), jnp.float32),
        ],
        compiler_params=params(10),
        cost_estimate=cost(0, 0, 0, 2 * recv.size),
        name="merge_x",
    )(recv, after)


def finish_kernel(*refs):
    cycle_ref, out_ref = refs[-2:]
    refs = refs[:-2]
    rows = JW // 16 * 8
    i_dev = rows // 8
    blocks = []
    for kind, _, tile_a in CHUNKS:
        count = tile_a * HALVES
        if kind == "z":
            recv_ref, refs = refs[0], refs[1:]
            sources, tiles = recv_ref.shape[:2]
            for tile in range(tiles):
                levels = [read_steps(recv_ref[s, tile, count * rows :, :]) for s in range(sources)]

                def summed(block, ref=recv_ref, tile=tile, levels=levels):
                    part = slice(block * rows, (block + 1) * rows)
                    return sum(
                        decode(ref[s, tile, part, :], levels[s][block : block + 1, :]) for s in range(len(levels))
                    )

                blocks += [functools.partial(summed, block) for block in range(count)]
        else:
            (keep_ref, recv_ref), refs = refs[:2], refs[2:]
            for tile in range(recv_ref.shape[0]):
                levels = read_steps(recv_ref[tile, count * rows :, :])

                def kept(block, keep=keep_ref, ref=recv_ref, tile=tile, levels=levels):
                    part = slice(block * rows, (block + 1) * rows)
                    return keep[tile, block] + decode(ref[tile, part, :], levels[block : block + 1, :])

                blocks += [functools.partial(kept, block) for block in range(count)]

    for group in range(AW // 8):

        @pl.when(pl.program_id(0) == group)
        def _group(group=group):
            for half in range(HALVES):
                totals = [blocks[(group * 8 + a) * HALVES + half]() for a in range(8)]
                for i in range(i_dev):
                    stack = jnp.stack([total[i * 8 : (i + 1) * 8, :] for total in totals], axis=0)
                    turned = jnp.swapaxes(stack, 0, 1)
                    for jj in range(8):
                        lanes = pl.ds(jj * BW + half * LANES, LANES)
                        out_ref[i, 0, :, lanes] = turned[jj] + cycle_ref[i, 0, :, lanes]


def finish(parts, cycle):
    shape = cycle.shape
    columns = shape[-1]
    block = pl.BlockSpec((shape[0], 1, 8, columns), lambda t: (0, t, 0, 0))
    out = pl.pallas_call(
        finish_kernel,
        grid=(AW // 8,),
        in_specs=[WHOLE] * len(parts) + [block],
        out_specs=block,
        out_shape=pltpu.HBM(shape, jnp.float32),
        compiler_params=params(12),
        cost_estimate=cost(0, 0, 0, 16 * cycle.size),
        name="finish",
    )(*[in_hbm(part) if part.dtype == jnp.float32 else in_vmem(part) for part in parts], cycle)
    return out.reshape(-1, columns)


def one_hot_places(virt):
    start = jnp.zeros(virt.shape, jnp.int32)
    for label in range(8):
        below = jnp.sum((virt < label).astype(jnp.int32), axis=1, keepdims=True)
        start = jnp.where(virt == label, below, start)
    place = lax.broadcasted_iota(jnp.int32, virt.shape, 1) - start
    return lax.broadcasted_iota(jnp.int32, (SEGMENT, BW), 0) == place


def spread_matrix(virt):
    hot = one_hot_places(virt).astype(jnp.float32)
    none = jnp.zeros_like(hot)
    group = LANES // SEGMENT
    rows = [jnp.concatenate([hot if a == b else none for b in range(group)], axis=1) for a in range(group)]
    return jnp.concatenate(rows, axis=0).astype(jnp.bfloat16)


def row_labels(occ, virt, first, rows):
    row = lax.broadcasted_iota(jnp.int32, (rows, 1), 0)
    k = first + row // PAN
    lane = lax.broadcasted_iota(jnp.int32, (rows, occ.shape[1]), 1)
    k_label = jnp.sum(jnp.where(lane == k, occ, 0), axis=1, keepdims=True)
    lane = lax.broadcasted_iota(jnp.int32, (rows, LANES), 1)
    c_label = jnp.sum(jnp.where(lane == row % PAN, virt[:, :LANES], 0), axis=1, keepdims=True)
    return k_label ^ c_label


def pack_kernel(occ_s_ref, occ_ref, virt_ref, cycle_ref, packed_ref, jb_ref):
    rows, columns = cycle_ref.shape
    virt = virt_ref[...]
    mine = row_labels(occ_ref[...], virt, lax.axis_index(OCC) * (rows // PAN), rows)
    spread = spread_matrix(virt)
    width = spread.shape[1]
    for step in range(columns // width):
        lanes = slice(step * width, (step + 1) * width)
        first = (lax.axis_index(VIR) * (columns // width) + step) * (width // BW)
        jb = jnp.concatenate([virt ^ occ_s_ref[first + jj] for jj in range(width // BW)], axis=1)
        jb_ref[:, lanes] = jb
        masked = jnp.where(mine == jb, cycle_ref[:, lanes], jnp.zeros((), jnp.bfloat16))
        packed_ref[:, step * LANES : (step + 1) * LANES] = lax.dot_general(
            masked, spread, (((1,), (1,)), ((), ())), preferred_element_type=jnp.float32
        ).astype(jnp.bfloat16)


def pack(occ_irrep, virt_irrep, cycle_int):
    rows, columns = cycle_int.shape
    width = columns * SEGMENT // BW
    return pl.pallas_call(
        pack_kernel,
        in_specs=[SCALARS, WHOLE, WHOLE, WHOLE],
        out_shape=[
            jax.ShapeDtypeStruct((rows, width), jnp.bfloat16),
            jax.ShapeDtypeStruct((1, columns), jnp.int32),
        ],
        compiler_params=params(12),
        cost_estimate=cost(rows, LANES, columns),
        name="pack",
    )(occ_irrep, occ_irrep[None, :], virt_irrep[None, :], in_hbm(cycle_int))


def lane_labels(occ_s, virt_s, depth):
    lane = lax.broadcasted_iota(jnp.int32, (1, LANES), 1)
    c_label = jnp.zeros((1, LANES), jnp.int32)
    for c in range(PAN):
        c_label = jnp.where(lane % PAN == c, virt_s[c], c_label)
    pieces = []
    per_row = LANES // PAN
    for row in range(depth // LANES):
        k_label = jnp.zeros((1, LANES), jnp.int32)
        for m in range(per_row):
            k_label = jnp.where(lane // PAN == m, occ_s[row * per_row + m], k_label)
        pieces.append(k_label ^ c_label)
    return jnp.concatenate(pieces, axis=1)


def cycle_kernel(occ_s_ref, virt_s_ref, virt_ref, jb_ref, amp_ref, packed_ref, _, out_ref, split_ref):
    rows, depth = amp_ref.shape
    width = LANES // SEGMENT * BW

    @pl.when(pl.program_id(0) == 0)
    def _split():
        label = lane_labels(occ_s_ref, virt_s_ref, depth)
        amp = amp_ref[...].astype(jnp.float32)
        for g in range(8):
            split_ref[g * rows : (g + 1) * rows, :] = jnp.where(label == g, amp, 0.0).astype(jnp.bfloat16)

    parts = jnp.dot(split_ref[...], packed_ref[...], preferred_element_type=jnp.float32)
    spread = spread_matrix(virt_ref[...]).astype(jnp.float32)
    for pair in range(packed_ref.shape[1] // LANES):
        lanes = slice(pair * LANES, (pair + 1) * LANES)
        wide = jnp.concatenate([parts[g * rows : (g + 1) * rows, lanes] for g in range(8)], axis=1)
        high = wide.astype(jnp.bfloat16)
        low = (wide - high.astype(jnp.float32)).astype(jnp.bfloat16)
        jb = jb_ref[:, pair * width : (pair + 1) * width]
        choose = jnp.concatenate([jnp.where(jb == g, spread, 0.0).astype(jnp.bfloat16) for g in range(8)], axis=0)
        both = jnp.dot(jnp.concatenate([high, low], axis=0), choose, preferred_element_type=jnp.float32)
        out_ref[..., pair * width : (pair + 1) * width] = (both[:rows, :] + both[rows:, :]).reshape(out_ref.shape[:3] + (width,))


def cycle_term(occ_irrep, virt_irrep, jb_irrep, amp, packed, after):
    rows, depth = amp.shape
    steps = 2
    columns = jb_irrep.shape[1]
    shape = (rows // AW, AW // 8, 8, columns)
    return pl.pallas_call(
        cycle_kernel,
        grid=(steps,),
        in_specs=[
            SCALARS,
            SCALARS,
            WHOLE,
            pl.BlockSpec((1, columns // steps), lambda t: (0, t)),
            pl.BlockSpec((rows, depth), lambda t: (0, 0)),
            pl.BlockSpec((depth, packed.shape[1] // steps), lambda t: (0, t)),
            ANYWHERE,
        ],
        out_specs=pl.BlockSpec(shape[:3] + (columns // steps,), lambda t: (0, 0, 0, t)),
        out_shape=pltpu.HBM(shape, jnp.float32),
        scratch_shapes=[pltpu.VMEM((8 * rows, depth), jnp.bfloat16)],
        compiler_params=params(28),
        cost_estimate=cost(2 * rows, depth, columns),
        name="cycle_term",
    )(in_hbm(occ_irrep), in_hbm(virt_irrep), virt_irrep[None, :], jb_irrep, in_hbm(amp), in_hbm(packed), after)


def swap(value, axis):
    return lax.ppermute(value, axis, [(0, 1), (1, 0)])


def exchange(value):
    return lax.all_to_all(value, "x", 0, 0)


def dense_cycle(amp, cycle_int, occ_irrep, virt_irrep, j_first, j_width):
    gathered = lax.all_gather(cycle_int, OCC, axis=0, tiled=True)
    kc_irrep = (occ_irrep[:, None] ^ virt_irrep[None, :PAN]).reshape(-1)
    jb_irrep = lax.dynamic_slice_in_dim(occ_irrep, j_first, j_width, 0)[:, None] ^ virt_irrep[None, :]
    allowed = kc_irrep[:, None] == jb_irrep.reshape(1, -1)
    masked = jnp.where(allowed, gathered, jnp.zeros((), gathered.dtype))
    cycle = jnp.dot(amp, masked, preferred_element_type=jnp.float32)
    return cycle.reshape(amp.shape[0] // AW, AW // 8, 8, -1)


def per_device(lam, ladder_int, cycle_amp, cycle_int, occ_irrep, virt_irrep):
    j_width = JW // lax.axis_size(VIR)
    j_first = lax.axis_index(VIR) * j_width
    fits = jnp.all(virt_irrep[SEGMENT:] != virt_irrep[:-SEGMENT])
    last, jb_irrep = pack(occ_irrep, virt_irrep, cycle_int)
    gathered = lax.all_gather(last, OCC, axis=0, tiled=True)

    kinds = [kind for kind, _, _ in CHUNKS]
    widths = [a * BW for _, a, _ in CHUNKS]
    tiles = [a * BW for _, _, a in CHUNKS]
    firsts = [sum(widths[:n]) for n in range(len(CHUNKS))]
    lam_rows = {}
    core_got, sent, kept, second = {}, {}, {}, {}

    def partner(n, last):
        if not lam_rows:
            last, lam_rows["own"], lam_rows["other"] = first_partner_part(
                lam, ladder_int, firsts[n], widths[n], tiles[n], last
            )
        else:
            last = partner_part(lam_rows["other"], ladder_int, firsts[n], widths[n], tiles[n], last)
        core_got[n] = swap(last, "core")
        return last

    def own(n, last):
        args = (lam_rows["own"], ladder_int, core_got[n], firsts[n], widths[n], tiles[n], last)
        if kinds[n] == "z":
            last, kept[n] = own_z_part(*args)
            sent[n] = swap(last, "z_hi")
        else:
            last = own_x_part(*args)
            sent[n] = exchange(last)
        return last

    def merge(n, last):
        if kinds[n] == "z":
            last = merge_z(kept[n], sent[n], last)
            second[n] = [exchange(last)]
        else:
            send, last = merge_x(sent[n], tiles[n] // LANES, last)
            second[n] = [last, swap(send, "z_hi")]
        return last

    for step in ORDER:
        if step == "C":
            cycle = lax.cond(
                fits,
                lambda gathered, jb, amp, own, occ, virt, last: cycle_term(occ, virt, jb, amp, gathered, last),
                lambda gathered, jb, amp, own, occ, virt, last: dense_cycle(amp, own, occ, virt, j_first, j_width),
                *(gathered, jb_irrep, cycle_amp, cycle_int, occ_irrep, virt_irrep, last),
            )
            last = cycle
        else:
            last = {"P": partner, "O": own, "M": merge}[step[0]](int(step[1]), last)
    return finish([part for n in range(len(CHUNKS)) for part in second[n]], cycle)


def solution(mesh):
    fine = Mesh(mesh.devices.reshape(2, 4, 4, 2, 2), ("z_lo", "y", "x", "z_hi", "core"))
    return jax.shard_map(
        per_device,
        mesh=fine,
        in_specs=(P(OCC, VIR), P(VIR, None), P(OCC, None), P(OCC, VIR), P(), P()),
        out_specs=P(OCC, VIR),
        check_vma=False,
    )
```
